32 devices in a mesh: row: 8 (over z, core), col: 4 (over y, x).
Axes of the slice: x: 2, y: 2, z: 4, core: 2. Of those that a mesh axis runs over, the one named last changes fastest.
Arguments:
- demo: bfloat16 [8192, 256], P(('row', 'col'))
- rollout: bfloat16 [8192, 256], P(('row', 'col'))
Outputs:
- demo_potential: float32 [8192], P(('row', 'col'))
- rollout_potential: float32 [8192], P(('row', 'col'))
- rollout_reward: float32 [8192], P(('row', 'col'))
All inputs are finite; a program needn't handle non-finite values.
Results may differ from the reference program's by a relative error of at most 0.0065.
The reference program's roundings to bfloat16 on the way (of `demo_unit` and `rollout_unit`) count: a program that leaves them out, or rounds other values in their place, can miss the bound.
Values may be sent and summed in bfloat16 or wider, within the bound.
A program may use at most 64 MiB of HBM per device.

```python
import math
import jax
import jax.numpy as jnp
from jax import lax

K = 256
ITERS = 2
N = 8192
M = 8192


def shared_parts(key):
    first = jax.random.fold_in(key, 0)
    base = jax.random.normal(first, (N, K), jnp.float32)
    return base


def draw_demo(key, part):
    base = shared_parts(key)
    return base.astype(jnp.bfloat16)


def draw_rollout(key, part):
    base = shared_parts(key)
    key = jax.random.fold_in(key, 23)
    first, second = jax.random.split(key, 2)
    picks = jax.random.randint(first, (M,), 0, N)
    noise = jax.random.normal(second, (M, K), jnp.float32)
    return (base[picks] + 0.6 * noise).astype(jnp.bfloat16)


def setup_inputs(seed: int = 0) -> dict:
    splits = jax.random.split(jax.random.key(seed), 3)
    demo = draw_demo(jax.random.fold_in(splits[2], 71), 0)
    rollout = draw_rollout(jax.random.fold_in(splits[2], 71), 0)
    return {"demo": demo, "rollout": rollout}


EPS = 0.005

def normalize(embed):
    values = embed.astype(jnp.float32)
    inverse = lax.rsqrt(lax.optimization_barrier(jnp.sum(values * values, axis=-1, keepdims=True)) + 1e-06)
    return (values * inverse).astype(jnp.bfloat16)

def cost_of(left, right):
    inner = lax.dot_general(left, right, (((1,), (1,)), ((), ())), preferred_element_type=jnp.float32)
    return 1.0 - inner

def reference(demo, rollout):
    demo_unit = normalize(demo)
    rollout_unit = normalize(rollout)
    total_rows = demo_unit.shape[0]
    total_cols = rollout_unit.shape[0]
    width = demo_unit.shape[1]
    block = min(512, total_rows)
    blocks = demo_unit.reshape(total_rows // block, block, width)
    log_rows = -math.log(total_rows)
    log_cols = -math.log(total_cols)
    g_pot = jnp.zeros((total_cols,), jnp.float32)
    f_pot = jnp.zeros((total_rows,), jnp.float32)
    for step in range(ITERS):

        def row_pass(demo_block):
            tile = cost_of(demo_block, rollout_unit)
            expo = (g_pot[None, :] - tile) / EPS
            top = lax.optimization_barrier(jnp.max(expo, axis=1))
            total = lax.optimization_barrier(jnp.sum(jnp.exp(expo - top[:, None]), axis=1))
            return EPS * log_rows - EPS * (top + jnp.log(total))
        f_pot = lax.map(row_pass, blocks).reshape(total_rows)
        f_blocks = f_pot.reshape(total_rows // block, block)

        def col_step(carry, item):
            top, total = carry
            demo_block, f_part = item
            tile = cost_of(demo_block, rollout_unit)
            expo = (f_part[:, None] - tile) / EPS
            newtop = jnp.maximum(top, lax.optimization_barrier(jnp.max(expo, axis=0)))
            total = total * jnp.exp(top - newtop) + lax.optimization_barrier(jnp.sum(jnp.exp(expo - newtop[None, :]), axis=0))
            return ((newtop, total), None)
        start = (jnp.full((total_cols,), -1e+30, jnp.float32), jnp.zeros((total_cols,), jnp.float32))
        (top, total), unused = lax.scan(col_step, start, (blocks, f_blocks))
        g_pot = EPS * log_cols - EPS * (top + jnp.log(total))
    f_blocks = f_pot.reshape(total_rows // block, block)

    def reward_step(carry, item):
        demo_block, f_part = item
        tile = cost_of(demo_block, rollout_unit)
        plan = jnp.exp((f_part[:, None] + g_pot[None, :] - tile) / EPS)
        return (carry + lax.optimization_barrier(jnp.sum(plan * tile, axis=0)), None)
    weighted, unused = lax.scan(reward_step, jnp.zeros((total_cols,), jnp.float32), (blocks, f_blocks))
    reward = -float(total_cols) * weighted
    return (f_pot / EPS, g_pot / EPS, reward)
```

```python
import functools
import math

import jax
import jax.numpy as jnp
from jax import lax
from jax.experimental import pallas as pl
from jax.experimental.pallas import tpu as pltpu
from jax.sharding import PartitionSpec as P

EPS = 0.005
MESH = pl.DeviceIdType.MESH
LANES = 128
SUB = 8


class Plan:
    def __init__(self, rows_axis, cols_axis, blk, width):
        self.core = 2
        depth = rows_axis // 2
        self.x = 1 << ((cols_axis.bit_length() - 1) // 2)
        self.y = cols_axis // self.x
        self.zl = min(depth, max(1, cols_axis // self.x))
        self.zh = depth // self.zl
        self.blk = blk
        self.width = width
        self.gr = self.zl * self.x
        self.gc = self.zh * self.y * self.core
        self.rows = self.gr * blk
        self.cols = self.gc * blk
        self.total = rows_axis * cols_axis * blk
        self.pieces = max(1, min(4, blk // 16))
        self.piece = blk // self.pieces


def normalize(embed):
    values = embed.astype(jnp.float32)
    inverse = lax.rsqrt(jnp.sum(values * values, axis=-1, keepdims=True) + 1e-06)
    return (values * inverse).astype(jnp.bfloat16)


def tree(op, items):
    items = list(items)
    while len(items) > 1:
        items = [
            op(items[i], items[i + 1]) if i + 1 < len(items) else items[i]
            for i in range(0, len(items), 2)
        ]
    return items[0]


def kernel(
    plan,
    demo_ref,
    roll_ref,
    fo_ref,
    go_ref,
    ro_ref,
    dem,
    rol,
    dist,
    kern,
    best,
    part,
    wide,
    scale,
    lf1,
    lf2,
    lg,
    f_own,
    g_own,
    cw_out,
    cw_in,
    s_dem,
    r_dem,
    s_rol,
    r_rol,
    s_f1,
    r_f1,
    s_f2,
    r_f2,
    s_g,
    r_g,
    s_c,
    r_c,
):
    blk, rows, cols = plan.blk, plan.rows, plan.cols
    n_parts = cols // LANES
    n_groups = rows // SUB
    row = lax.axis_index("row")
    col = lax.axis_index("col")
    core, z = lax.rem(row, 2), row // 2
    zlo, zhi = lax.rem(z, plan.zl), z // plan.zl
    x, y = lax.rem(col, plan.x), col // plan.x

    def row_peer(dz, dx):
        zz, xx = lax.rem(zlo + dz, plan.zl), lax.rem(x + dx, plan.x)
        device = ((zhi * plan.zl + zz) * 2 + core, y * plan.x + xx)
        return device, zz * plan.x + xx

    def col_peer(dz, dy, dc):
        zz, yy, cc = lax.rem(zhi + dz, plan.zh), lax.rem(y + dy, plan.y), lax.rem(core + dc, 2)
        device = ((zz * plan.zl + zlo) * 2 + cc, yy * plan.x + x)
        return device, (zz * plan.y + yy) * 2 + cc

    row_offsets = [(a, b) for a in range(plan.zl) for b in range(plan.x)]
    col_offsets = [(a, b, c) for a in range(plan.zh) for b in range(plan.y) for c in range(2)]
    row_peers = {o: row_peer(*o) for o in row_offsets}
    col_peers = {o: col_peer(*o) for o in col_offsets}
    p_me = row_peers[(0, 0)][1]
    q_me = col_peers[(0, 0, 0)][1]
    row_others = [row_peers[o] for o in row_offsets[1:]]
    col_others = [col_peers[o] for o in col_offsets[1:]]

    barrier = pltpu.get_barrier_semaphore()
    for device, _ in row_others + col_others:
        pl.semaphore_signal(barrier, inc=1, device_id=device, device_id_type=MESH)

    def slot(buf, index, piece):
        start = pl.multiple_of(index * blk + piece * plan.piece, 16)
        return buf.at[pl.ds(start, plan.piece), :]

    dem[pl.ds(pl.multiple_of(p_me * blk, 16), blk), :] = normalize(demo_ref[...])
    rol[pl.ds(pl.multiple_of(q_me * blk, 16), blk), :] = normalize(roll_ref[...])
    pl.semaphore_wait(barrier, len(row_others) + len(col_others))

    partner = col_peers[(0, 0, 1)][0]
    started = []

    def send(buf, index, piece, device, ssem, rsem, count):
        ref = slot(buf, index, piece)
        copy = pltpu.make_async_remote_copy(
            src_ref=ref,
            dst_ref=ref,
            send_sem=ssem.at[count[0]],
            recv_sem=rsem.at[index, piece],
            device_id=device,
            device_id_type=MESH,
        )
        copy.start()
        count[0] += 1
        started.append(copy)

    def arrived(buf, index, piece, ssem, rsem):
        ref = slot(buf, index, piece)
        pltpu.make_async_remote_copy(
            src_ref=ref,
            dst_ref=ref,
            send_sem=ssem.at[0],
            recv_sem=rsem.at[index, piece],
            device_id=partner,
            device_id_type=MESH,
        ).wait_recv()

    n_dem, n_rol = [0], [0]
    send_dem = lambda i, k, d: send(dem, i, k, d, s_dem, r_dem, n_dem)
    send_rol = lambda i, k, d: send(rol, i, k, d, s_rol, r_rol, n_rol)
    for k in range(plan.pieces):
        for dz in range(1, plan.zl):
            send_dem(p_me, k, row_peers[(dz, 0)][0])
        for dz in range(1, plan.zh):
            send_rol(q_me, k, col_peers[(dz, 0, 0)][0])
        for dx in range(1, plan.x):
            send_dem(p_me, k, row_peers[(0, dx)][0])
        for dy in range(1, plan.y):
            send_rol(q_me, k, col_peers[(0, dy, 0)][0])
        send_rol(q_me, k, col_peers[(0, 0, 1)][0])
    for k in range(plan.pieces):
        for dz in range(1, plan.zl):
            index = row_peers[(dz, 0)][1]
            arrived(dem, index, k, s_dem, r_dem)
            for dx in range(1, plan.x):
                send_dem(index, k, row_peers[(0, dx)][0])
        for dz in range(1, plan.zh):
            index = col_peers[(dz, 0, 0)][1]
            arrived(rol, index, k, s_rol, r_rol)
            for dy in range(1, plan.y):
                send_rol(index, k, col_peers[(0, dy, 0)][0])
            send_rol(index, k, partner)
        for dy in range(1, plan.y):
            index = col_peers[(0, dy, 0)][1]
            arrived(rol, index, k, s_rol, r_rol)
            send_rol(index, k, partner)
    for k in range(plan.pieces):
        for dz in range(1, plan.zh):
            for dy in range(1, plan.y):
                index = col_peers[(dz, dy, 0)][1]
                arrived(rol, index, k, s_rol, r_rol)
                send_rol(index, k, partner)
    for k in range(plan.pieces):
        for dz in range(plan.zl):
            for dx in range(1, plan.x):
                arrived(dem, row_peers[(dz, dx)][1], k, s_dem, r_dem)
        for dz in range(plan.zh):
            for dy in range(plan.y):
                arrived(rol, col_peers[(dz, dy, 1)][1], k, s_rol, r_rol)

    step = 2 * LANES
    for c in range(cols // step):
        inner = lax.dot_general(
            dem[...],
            rol[c * step : (c + 1) * step, :],
            (((1,), (1,)), ((), ())),
            preferred_element_type=jnp.float32,
        )
        dist[:, c * step : (c + 1) * step] = (1.0 - inner) * (1.0 / EPS)

    def lanes(c):
        return slice(c * LANES, (c + 1) * LANES)

    def group(r):
        return pl.ds(pl.multiple_of(r * SUB, SUB), SUB)

    eye = lax.broadcasted_iota(jnp.int32, (LANES, LANES), 0) == lax.broadcasted_iota(
        jnp.int32, (LANES, LANES), 1
    )

    def to_lanes(column):
        return jnp.sum(jnp.where(eye, column, 0.0), axis=0, keepdims=True)

    def spread(line):
        for k in range(rows // LANES):
            column = jnp.sum(jnp.where(eye, line[:, lanes(k)], 0.0), axis=1, keepdims=True)
            wide[lanes(k), :] = jnp.broadcast_to(column, (LANES, LANES))

    def exchange(buf, index, others, ssem, rsem):
        copies = [
            pltpu.make_async_remote_copy(
                src_ref=buf.at[index],
                dst_ref=buf.at[index],
                send_sem=ssem.at[i],
                recv_sem=rsem.at[index],
                device_id=device,
                device_id_type=MESH,
            )
            for i, (device, _) in enumerate(others)
        ]
        for copy in copies:
            copy.start()
        started.extend(copies)
        for i, (device, other) in enumerate(others):
            pltpu.make_async_remote_copy(
                src_ref=buf.at[other],
                dst_ref=buf.at[other],
                send_sem=ssem.at[i],
                recv_sem=rsem.at[other],
                device_id=device,
                device_id_type=MESH,
            ).wait_recv()

    def log_total(buf, count):
        values = [buf[i] for i in range(count)]
        top = tree(jnp.maximum, values)
        return top + jnp.log(tree(jnp.add, [jnp.exp(v - top) for v in values]))

    log_n = math.log(plan.total)

    def first_rows(r, carry):
        here = group(r)
        values = [dist[here, lanes(c)] for c in range(n_parts)]
        low = tree(jnp.minimum, values)
        best[here, :] = low
        part[here, :] = tree(jnp.add, [jnp.exp(low - v) for v in values])
        return carry

    lax.fori_loop(0, n_groups, first_rows, 0, unroll=4)
    for k in range(rows // LANES):
        low = best[lanes(k), :]
        least = jnp.min(low, axis=1, keepdims=True)
        total = jnp.sum(part[lanes(k), :] * jnp.exp(least - low), axis=1, keepdims=True)
        lf1[p_me, :, lanes(k)] = jnp.log(to_lanes(total)) - to_lanes(least)
    exchange(lf1, p_me, row_others, s_f1, r_f1)
    f_line = -log_n - log_total(lf1, plan.gr)
    spread(f_line)

    def col_max(r, carry):
        here = group(r)
        f_here = wide[here, :]
        return tuple(
            jnp.maximum(carry[c], f_here - dist[here, lanes(c)]) for c in range(n_parts)
        )

    tops = lax.fori_loop(
        0,
        n_groups,
        col_max,
        tuple(jnp.full((SUB, LANES), -jnp.inf, jnp.float32) for _ in range(n_parts)),
        unroll=4,
    )

    def col_sum(r, carry):
        here = group(r)
        f_here = wide[here, :]
        out = []
        for c in range(n_parts):
            value = jnp.exp((f_here - dist[here, lanes(c)]) - tops[c])
            kern[here, lanes(c)] = value
            out.append(carry[c] + value)
        return tuple(out)

    zeros = tuple(jnp.zeros((SUB, LANES), jnp.float32) for _ in range(n_parts))
    sums = lax.fori_loop(0, n_groups, col_sum, zeros, unroll=4)
    for c in range(n_parts):
        top = jnp.max(tops[c], axis=0, keepdims=True)
        total = jnp.sum(sums[c] * jnp.exp(tops[c] - top), axis=0, keepdims=True)
        lg[q_me, :, lanes(c)] = top + jnp.log(total)
    exchange(lg, q_me, col_others, s_g, r_g)
    g_line = -log_n - log_total(lg, plan.gc)
    for c in range(n_parts):
        scale[:, lanes(c)] = jnp.exp(tops[c] + g_line[:, lanes(c)])

    def second_rows(r, carry):
        here = group(r)
        part[here, :] = tree(
            jnp.add, [kern[here, lanes(c)] * scale[:, lanes(c)] for c in range(n_parts)]
        )
        return carry

    lax.fori_loop(0, n_groups, second_rows, 0, unroll=4)
    for k in range(rows // LANES):
        lf2[p_me, :, lanes(k)] = to_lanes(jnp.sum(part[lanes(k), :], axis=1, keepdims=True))
    exchange(lf2, p_me, row_others, s_f2, r_f2)
    mass = tree(jnp.add, [lf2[i] for i in range(plan.gr)]) * float(plan.total)
    spread(1.0 / mass)
    f_line = f_line - jnp.log(mass)
    for i in range(plan.gr):
        f_own[i] = f_line[:, i * blk : (i + 1) * blk]
    for i in range(plan.gc):
        g_own[i] = g_line[:, i * blk : (i + 1) * blk]

    def last(r, carry):
        here = group(r)
        u_here = wide[here, :]
        mass_c, cost_c = carry
        new_mass, new_cost = [], []
        for c in range(n_parts):
            value = u_here * kern[here, lanes(c)]
            new_mass.append(mass_c[c] + value)
            new_cost.append(cost_c[c] + value * dist[here, lanes(c)])
        return tuple(new_mass), tuple(new_cost)

    mass_c, cost_c = lax.fori_loop(0, n_groups, last, (zeros, zeros), unroll=2)

    def finish(values):
        return jnp.concatenate(
            [
                jnp.sum(values[c] * scale[:, lanes(c)], axis=0, keepdims=True)
                for c in range(n_parts)
            ],
            axis=1,
        )

    both = jnp.concatenate([finish(mass_c), finish(cost_c)], axis=0)
    for i in range(plan.gc):
        cw_out[i] = both[:, i * blk : (i + 1) * blk]
    copies = [
        pltpu.make_async_remote_copy(
            src_ref=cw_out.at[other],
            dst_ref=cw_in.at[q_me],
            send_sem=s_c.at[i],
            recv_sem=r_c.at[q_me],
            device_id=device,
            device_id_type=MESH,
        )
        for i, (device, other) in enumerate(col_others)
    ]
    for copy in copies:
        copy.start()
    started.extend(copies)
    cw_in[q_me] = cw_out[q_me]
    for i, (device, other) in enumerate(col_others):
        pltpu.make_async_remote_copy(
            src_ref=cw_out.at[other],
            dst_ref=cw_in.at[other],
            send_sem=s_c.at[i],
            recv_sem=r_c.at[other],
            device_id=device,
            device_id_type=MESH,
        ).wait_recv()
    total = tree(jnp.add, [cw_in[i] for i in range(plan.gc)])
    fo_ref[...] = f_own[p_me]
    go_ref[...] = g_own[q_me] - jnp.log(total[0:1] * float(plan.total))
    ro_ref[...] = total[1:2] / total[0:1] * -EPS
    for copy in started:
        copy.wait_send()


def body(plan, demo, rollout):
    blk, width, rows, cols = plan.blk, plan.width, plan.rows, plan.cols
    n_dem = plan.pieces * ((plan.zl - 1) + (plan.x - 1) * plan.zl)
    n_rol = plan.pieces * (
        (plan.zh - 1) + (plan.y - 1) * plan.zh + plan.zh * plan.y
    )
    dma = pltpu.SemaphoreType.DMA
    f32 = jnp.float32
    outs = pl.pallas_call(
        functools.partial(kernel, plan),
        out_shape=[jax.ShapeDtypeStruct((1, blk), f32)] * 3,
        in_specs=[pl.BlockSpec(memory_space=pltpu.VMEM)] * 2,
        out_specs=[pl.BlockSpec(memory_space=pltpu.VMEM)] * 3,
        scratch_shapes=[
            pltpu.VMEM((rows, width), jnp.bfloat16),
            pltpu.VMEM((cols, width), jnp.bfloat16),
            pltpu.VMEM((rows, cols), f32),
            pltpu.VMEM((rows, cols), f32),
            pltpu.VMEM((rows, LANES), f32),
            pltpu.VMEM((rows, LANES), f32),
            pltpu.VMEM((rows, LANES), f32),
            pltpu.VMEM((SUB, cols), f32),
            pltpu.VMEM((plan.gr, 1, rows), f32),
            pltpu.VMEM((plan.gr, 1, rows), f32),
            pltpu.VMEM((plan.gc, 1, cols), f32),
            pltpu.VMEM((plan.gr, 1, blk), f32),
            pltpu.VMEM((plan.gc, 1, blk), f32),
            pltpu.VMEM((plan.gc, 2, blk), f32),
            pltpu.VMEM((plan.gc, 2, blk), f32),
            dma((n_dem,)),
            dma((plan.gr, plan.pieces)),
            dma((n_rol,)),
            dma((plan.gc, plan.pieces)),
            dma((plan.gr,)),
            dma((plan.gr,)),
            dma((plan.gr,)),
            dma((plan.gr,)),
            dma((plan.gc,)),
            dma((plan.gc,)),
            dma((plan.gc,)),
            dma((plan.gc,)),
        ],
        compiler_params=pltpu.CompilerParams(
            collective_id=0, has_side_effects=True, vmem_limit_bytes=48 * 1024 * 1024
        ),
    )(demo, rollout)
    return tuple(o.reshape(blk) for o in outs)


def solution(mesh):
    rows_axis, cols_axis = mesh.shape["row"], mesh.shape["col"]

    def run(demo, rollout):
        blk = demo.shape[0] // (rows_axis * cols_axis)
        plan = Plan(rows_axis, cols_axis, blk, demo.shape[1])
        return jax.shard_map(
            functools.partial(body, plan),
            mesh=mesh,
            in_specs=(P(("row", "col"), None), P(("row", "col"), None)),
            out_specs=(P(("row", "col")), P(("row", "col")), P(("row", "col"))),
            check_vma=False,
        )(demo, rollout)

    return run
```

```python
import functools
import math

import jax
import jax.numpy as jnp
from jax import lax
from jax.experimental import pallas as pl
from jax.experimental.pallas import tpu as pltpu
from jax.sharding import PartitionSpec as P

EPS = 0.005
MESH = pl.DeviceIdType.MESH
LANES = 128
SUB = 8


class Plan:
    def __init__(self, rows_axis, cols_axis, blk, width):
        self.core = 2
        depth = rows_axis // 2
        self.x = 1 << ((cols_axis.bit_length() - 1) // 2)
        self.y = cols_axis // self.x
        self.zl = min(depth, max(1, cols_axis // self.x))
        self.zh = depth // self.zl
        self.blk = blk
        self.width = width
        self.gr = self.zl * self.x
        self.gc = self.zh * self.y * self.core
        self.rows = self.gr * blk
        self.cols = self.gc * blk
        self.total = rows_axis * cols_axis * blk
        self.pieces = max(1, min(4, blk // 16))
        self.piece = blk // self.pieces
        self.chunks = 4 if blk % LANES == 0 and self.gr % 4 == 0 else 1


def normalize(embed):
    values = embed.astype(jnp.float32)
    inverse = lax.rsqrt(jnp.sum(values * values, axis=-1, keepdims=True) + 1e-06)
    return (values * inverse).astype(jnp.bfloat16)


def tree(op, items):
    items = list(items)
    while len(items) > 1:
        items = [
            op(items[i], items[i + 1]) if i + 1 < len(items) else items[i]
            for i in range(0, len(items), 2)
        ]
    return items[0]


def kernel(
    plan,
    demo_hbm,
    roll_hbm,
    out_ref,
    demo_ref,
    roll_ref,
    dem,
    rol,
    dist,
    kern,
    best,
    part,
    wide,
    scale,
    lf1,
    lf2,
    lg,
    f_all,
    g_all,
    cw_out,
    cw_in,
    s_in,
    s_dem,
    r_dem,
    s_rol,
    r_rol,
    s_f1,
    r_f1,
    s_f2,
    r_f2,
    s_g,
    r_g,
    s_c,
    r_c,
):
    blk, rows, cols = plan.blk, plan.rows, plan.cols
    n_parts = cols // LANES
    chunks, chunk = plan.chunks, rows // plan.chunks
    row = lax.axis_index("row")
    col = lax.axis_index("col")
    core, z = lax.rem(row, 2), row // 2
    zlo, zhi = lax.rem(z, plan.zl), z // plan.zl
    x, y = lax.rem(col, plan.x), col // plan.x

    load_demo = pltpu.make_async_copy(demo_hbm, demo_ref, s_in.at[0])
    load_roll = pltpu.make_async_copy(roll_hbm, roll_ref, s_in.at[1])
    load_demo.start()
    load_roll.start()

    def row_peer(dz, dx):
        zz, xx = lax.rem(zlo + dz, plan.zl), lax.rem(x + dx, plan.x)
        device = ((zhi * plan.zl + zz) * 2 + core, y * plan.x + xx)
        return device, zz * plan.x + xx

    def col_peer(dz, dy, dc):
        zz, yy, cc = lax.rem(zhi + dz, plan.zh), lax.rem(y + dy, plan.y), lax.rem(core + dc, 2)
        device = ((zz * plan.zl + zlo) * 2 + cc, yy * plan.x + x)
        return device, (zz * plan.y + yy) * 2 + cc

    row_offsets = [(a, b) for a in range(plan.zl) for b in range(plan.x)]
    col_offsets = [(a, b, c) for a in range(plan.zh) for b in range(plan.y) for c in range(2)]
    row_peers = {o: row_peer(*o) for o in row_offsets}
    col_peers = {o: col_peer(*o) for o in col_offsets}
    p_me = row_peers[(0, 0)][1]
    q_me = col_peers[(0, 0, 0)][1]
    row_others = [row_peers[o] for o in row_offsets[1:]]
    col_others = [col_peers[o] for o in col_offsets[1:]]
    places = [col_peers[o][1] for o in col_offsets]

    barrier = pltpu.get_barrier_semaphore()
    for device, _ in row_others + col_others:
        pl.semaphore_signal(barrier, inc=1, device_id=device, device_id_type=MESH)

    def slot(buf, index, piece):
        start = pl.multiple_of(index * blk + piece * plan.piece, 16)
        return buf.at[pl.ds(start, plan.piece), :]

    load_demo.wait()
    dem[pl.ds(pl.multiple_of(p_me * blk, 16), blk), :] = normalize(demo_ref[...])
    load_roll.wait()
    rol[pl.ds(pl.multiple_of(q_me * blk, 16), blk), :] = normalize(roll_ref[...])
    pl.semaphore_wait(barrier, len(row_others) + len(col_others))

    partner = col_peers[(0, 0, 1)][0]
    started = []

    def send(buf, index, piece, device, ssem, rsem, count):
        ref = slot(buf, index, piece)
        copy = pltpu.make_async_remote_copy(
            src_ref=ref,
            dst_ref=ref,
            send_sem=ssem.at[count[0]],
            recv_sem=rsem.at[index, piece],
            device_id=device,
            device_id_type=MESH,
        )
        copy.start()
        count[0] += 1
        started.append(copy)

    def arrived(buf, index, piece, ssem, rsem):
        ref = slot(buf, index, piece)
        pltpu.make_async_remote_copy(
            src_ref=ref,
            dst_ref=ref,
            send_sem=ssem.at[0],
            recv_sem=rsem.at[index, piece],
            device_id=partner,
            device_id_type=MESH,
        ).wait_recv()

    n_dem, n_rol = [0], [0]
    send_dem = lambda i, k, d: send(dem, i, k, d, s_dem, r_dem, n_dem)
    send_rol = lambda i, k, d: send(rol, i, k, d, s_rol, r_rol, n_rol)
    for k in range(plan.pieces):
        for dz in range(1, plan.zl):
            send_dem(p_me, k, row_peers[(dz, 0)][0])
        for dz in range(1, plan.zh):
            send_rol(q_me, k, col_peers[(dz, 0, 0)][0])
        for dx in range(1, plan.x):
            send_dem(p_me, k, row_peers[(0, dx)][0])
        for dy in range(1, plan.y):
            send_rol(q_me, k, col_peers[(0, dy, 0)][0])
        send_rol(q_me, k, partner)
    for k in range(plan.pieces):
        for dz in range(1, plan.zl):
            index = row_peers[(dz, 0)][1]
            arrived(dem, index, k, s_dem, r_dem)
            for dx in range(1, plan.x):
                send_dem(index, k, row_peers[(0, dx)][0])
        for dz in range(1, plan.zh):
            index = col_peers[(dz, 0, 0)][1]
            arrived(rol, index, k, s_rol, r_rol)
            for dy in range(1, plan.y):
                send_rol(index, k, col_peers[(0, dy, 0)][0])
            send_rol(index, k, partner)
        for dy in range(1, plan.y):
            index = col_peers[(0, dy, 0)][1]
            arrived(rol, index, k, s_rol, r_rol)
            send_rol(index, k, partner)
    for k in range(plan.pieces):
        for dz in range(plan.zl):
            for dx in range(1, plan.x):
                arrived(dem, row_peers[(dz, dx)][1], k, s_dem, r_dem)

    def lanes(c):
        return slice(c * LANES, (c + 1) * LANES)

    def group(r):
        return pl.ds(pl.multiple_of(r * SUB, SUB), SUB)

    def over(h, body, init, unroll):
        first = h * chunk // SUB
        return lax.fori_loop(first, first + chunk // SUB, body, init, unroll=unroll)

    eye = lax.broadcasted_iota(jnp.int32, (LANES, LANES), 0) == lax.broadcasted_iota(
        jnp.int32, (LANES, LANES), 1
    )

    def to_lanes(column):
        return jnp.sum(jnp.where(eye, column, 0.0), axis=0, keepdims=True)

    def tile(where, count):
        for i in range(where, where + count):
            inner = lax.dot_general(
                dem[...],
                rol[pl.ds(pl.multiple_of(places[i] * blk, 16), blk), :],
                (((1,), (1,)), ((), ())),
                preferred_element_type=jnp.float32,
            )
            dist[:, i * blk : (i + 1) * blk] = (1.0 - inner) * (1.0 / EPS)

    def row_stats(h, first, count, fresh):
        def step(r, carry):
            here = group(r)
            values = [dist[here, lanes(c)] for c in range(first, first + count)]
            low = tree(jnp.minimum, values)
            if not fresh:
                before = best[here, :]
                low = jnp.minimum(low, before)
            total = tree(jnp.add, [jnp.exp(low - v) for v in values])
            if not fresh:
                total = total + part[here, :] * jnp.exp(low - before)
            best[here, :] = low
            part[here, :] = total
            return carry

        over(h, step, 0, 4)

    def store_line(buf, index, k, line):
        at = k * LANES
        done = 0
        while done < LANES:
            i, j = (at + done) // blk, (at + done) % blk
            n = min(LANES - done, blk - j)
            buf[index, i : i + 1, j : j + n] = line[:, done : done + n]
            done += n

    def exchange_start(buf, index, others, ssem, rsem, h, slots):
        here = pl.ds(h * slots, slots)
        for i, (device, _) in enumerate(others):
            copy = pltpu.make_async_remote_copy(
                src_ref=buf.at[index, here],
                dst_ref=buf.at[index, here],
                send_sem=ssem.at[i, h],
                recv_sem=rsem.at[index, h],
                device_id=device,
                device_id_type=MESH,
            )
            copy.start()
            started.append(copy)

    def exchange_wait(buf, others, ssem, rsem, h, slots):
        here = pl.ds(h * slots, slots)
        for i, (device, other) in enumerate(others):
            pltpu.make_async_remote_copy(
                src_ref=buf.at[other, here],
                dst_ref=buf.at[other, here],
                send_sem=ssem.at[i, h],
                recv_sem=rsem.at[other, h],
                device_id=device,
                device_id_type=MESH,
            ).wait_recv()

    def log_total(values):
        top = tree(jnp.maximum, values)
        return top + jnp.log(tree(jnp.add, [jnp.exp(v - top) for v in values]))

    def line_of(pieces):
        return pieces[0] if len(pieces) == 1 else jnp.concatenate(pieces, axis=1)

    def spread(h, values):
        line = line_of([values[i : i + 1, :] for i in range(values.shape[0])])
        for k in range(chunk // LANES):
            column = jnp.sum(jnp.where(eye, line[:, lanes(k)], 0.0), axis=1, keepdims=True)
            wide[lanes(h * (chunk // LANES) + k), :] = jnp.broadcast_to(column, (LANES, LANES))

    per_chunk = chunk // LANES
    slots = chunk // blk
    log_n = math.log(plan.total)

    every = [o for o in col_offsets if o[2] == 0]
    fresh = True
    done = 0
    for at, (dz, dy, _) in enumerate(every):
        if dz > 0 and dy > 0:
            for k in range(plan.pieces):
                index = col_peers[(dz, dy, 0)][1]
                arrived(rol, index, k, s_rol, r_rol)
                send_rol(index, k, partner)
        for k in range(plan.pieces):
            arrived(rol, col_peers[(dz, dy, 1)][1], k, s_rol, r_rol)
        tile(2 * at, 2)
        if (2 * (at + 1) * blk) % LANES == 0 and at + 1 < len(every):
            upto = 2 * (at + 1) * blk // LANES
            for h in range(chunks):
                row_stats(h, done, upto - done, fresh)
            fresh, done = False, upto
    for h in range(chunks):
        row_stats(h, done, n_parts - done, fresh)
        for k in range(h * per_chunk, (h + 1) * per_chunk):
            low = best[lanes(k), :]
            least = jnp.min(low, axis=1, keepdims=True)
            total = jnp.sum(part[lanes(k), :] * jnp.exp(least - low), axis=1, keepdims=True)
            store_line(lf1, p_me, k, jnp.log(to_lanes(total)) - to_lanes(least))
        exchange_start(lf1, p_me, row_others, s_f1, r_f1, h, slots)

    def col_max(r, carry):
        here = group(r)
        f_here = wide[here, :]
        return tuple(
            jnp.maximum(carry[c], f_here - dist[here, lanes(c)]) for c in range(n_parts)
        )

    tops = tuple(jnp.full((SUB, LANES), -jnp.inf, jnp.float32) for _ in range(n_parts))
    for h in range(chunks):
        exchange_wait(lf1, row_others, s_f1, r_f1, h, slots)
        here = pl.ds(h * slots, slots)
        f_all[here, :] = -log_n - log_total([lf1[i, here, :] for i in range(plan.gr)])
        spread(h, f_all[here, :])
        tops = over(h, col_max, tops, 4)

    def col_sum(r, carry):
        here = group(r)
        f_here = wide[here, :]
        out = []
        for c in range(n_parts):
            value = jnp.exp((f_here - dist[here, lanes(c)]) - tops[c])
            kern[here, lanes(c)] = value
            out.append(carry[c] + value)
        return tuple(out)

    zeros = tuple(jnp.zeros((SUB, LANES), jnp.float32) for _ in range(n_parts))
    sums = lax.fori_loop(0, rows // SUB, col_sum, zeros, unroll=4)
    pieces = []
    for c in range(n_parts):
        top = jnp.max(tops[c], axis=0, keepdims=True)
        total = jnp.sum(sums[c] * jnp.exp(tops[c] - top), axis=0, keepdims=True)
        pieces.append(top + jnp.log(total))
    line = line_of(pieces)
    for i, place in enumerate(places):
        lg[q_me, pl.ds(place, 1), :] = line[:, i * blk : (i + 1) * blk]
    exchange_start(lg, q_me, col_others, s_g, r_g, 0, plan.gc)
    exchange_wait(lg, col_others, s_g, r_g, 0, plan.gc)
    g_all[...] = -log_n - log_total([lg[i] for i in range(plan.gc)])
    g_line = line_of([g_all[pl.ds(place, 1), :] for place in places])
    for c in range(n_parts):
        scale[:, lanes(c)] = jnp.exp(tops[c] + g_line[:, lanes(c)])

    def second_rows(r, carry):
        here = group(r)
        part[here, :] = tree(
            jnp.add, [kern[here, lanes(c)] * scale[:, lanes(c)] for c in range(n_parts)]
        )
        return carry

    for h in range(chunks):
        over(h, second_rows, 0, 4)
        for k in range(h * per_chunk, (h + 1) * per_chunk):
            total = jnp.sum(part[lanes(k), :], axis=1, keepdims=True)
            store_line(lf2, p_me, k, to_lanes(total))
        exchange_start(lf2, p_me, row_others, s_f2, r_f2, h, slots)

    def last(r, carry):
        here = group(r)
        u_here = wide[here, :]
        mass_c, cost_c = carry
        new_mass, new_cost = [], []
        for c in range(n_parts):
            value = u_here * kern[here, lanes(c)]
            new_mass.append(mass_c[c] + value)
            new_cost.append(cost_c[c] + value * dist[here, lanes(c)])
        return tuple(new_mass), tuple(new_cost)

    both = (zeros, zeros)
    for h in range(chunks):
        exchange_wait(lf2, row_others, s_f2, r_f2, h, slots)
        here = pl.ds(h * slots, slots)
        mass = tree(jnp.add, [lf2[i, here, :] for i in range(plan.gr)]) * float(plan.total)
        spread(h, 1.0 / mass)
        f_all[here, :] = f_all[here, :] - jnp.log(mass)
        both = over(h, last, both, 2)

    def finish(values):
        return line_of(
            [
                jnp.sum(values[c] * scale[:, lanes(c)], axis=0, keepdims=True)
                for c in range(n_parts)
            ]
        )

    both = jnp.concatenate([finish(both[0]), finish(both[1])], axis=0)
    for i, place in enumerate(places):
        cw_out[place] = both[:, i * blk : (i + 1) * blk]
    for i, (device, other) in enumerate(col_others):
        copy = pltpu.make_async_remote_copy(
            src_ref=cw_out.at[other],
            dst_ref=cw_in.at[q_me],
            send_sem=s_c.at[i],
            recv_sem=r_c.at[q_me],
            device_id=device,
            device_id_type=MESH,
        )
        copy.start()
        started.append(copy)
    cw_in[q_me] = cw_out[q_me]
    for i, (device, other) in enumerate(col_others):
        pltpu.make_async_remote_copy(
            src_ref=cw_out.at[other],
            dst_ref=cw_in.at[other],
            send_sem=s_c.at[i],
            recv_sem=r_c.at[other],
            device_id=device,
            device_id_type=MESH,
        ).wait_recv()
    total = tree(jnp.add, [cw_in[i] for i in range(plan.gc)])
    out_ref[0:1, :] = f_all[pl.ds(p_me, 1), :]
    out_ref[1:2, :] = g_all[pl.ds(q_me, 1), :] - jnp.log(total[0:1] * float(plan.total))
    out_ref[2:3, :] = total[1:2] / total[0:1] * -EPS
    for copy in started:
        copy.wait_send()


def body(plan, demo, rollout):
    blk, width, rows, cols = plan.blk, plan.width, plan.rows, plan.cols
    n_dem = plan.pieces * ((plan.zl - 1) + (plan.x - 1) * plan.zl)
    n_rol = plan.pieces * (
        (plan.zh - 1) + (plan.y - 1) * plan.zh + plan.zh * plan.y
    )
    dma = pltpu.SemaphoreType.DMA
    f32 = jnp.float32
    out = pl.pallas_call(
        functools.partial(kernel, plan),
        out_shape=jax.ShapeDtypeStruct((3, blk), f32),
        in_specs=[pl.BlockSpec(memory_space=pltpu.HBM)] * 2,
        out_specs=pl.BlockSpec(memory_space=pltpu.VMEM),
        scratch_shapes=[
            pltpu.VMEM((blk, width), jnp.bfloat16),
            pltpu.VMEM((blk, width), jnp.bfloat16),
            pltpu.VMEM((rows, width), jnp.bfloat16),
            pltpu.VMEM((cols, width), jnp.bfloat16),
            pltpu.VMEM((rows, cols), f32),
            pltpu.VMEM((rows, cols), f32),
            pltpu.VMEM((rows, LANES), f32),
            pltpu.VMEM((rows, LANES), f32),
            pltpu.VMEM((rows, LANES), f32),
            pltpu.VMEM((SUB, cols), f32),
            pltpu.VMEM((plan.gr, plan.gr, blk), f32),
            pltpu.VMEM((plan.gr, plan.gr, blk), f32),
            pltpu.VMEM((plan.gc, plan.gc, blk), f32),
            pltpu.VMEM((plan.gr, blk), f32),
            pltpu.VMEM((plan.gc, blk), f32),
            pltpu.VMEM((plan.gc, 2, blk), f32),
            pltpu.VMEM((plan.gc, 2, blk), f32),
            dma((2,)),
            dma((n_dem,)),
            dma((plan.gr, plan.pieces)),
            dma((n_rol,)),
            dma((plan.gc, plan.pieces)),
            dma((plan.gr, plan.chunks)),
            dma((plan.gr, plan.chunks)),
            dma((plan.gr, plan.chunks)),
            dma((plan.gr, plan.chunks)),
            dma((plan.gc, 1)),
            dma((plan.gc, 1)),
            dma((plan.gc,)),
            dma((plan.gc,)),
        ],
        compiler_params=pltpu.CompilerParams(
            collective_id=0, has_side_effects=True, vmem_limit_bytes=48 * 1024 * 1024
        ),
    )(demo, rollout)
    return out[0], out[1], out[2]


def solution(mesh):
    rows_axis, cols_axis = mesh.shape["row"], mesh.shape["col"]

    def run(demo, rollout):
        blk = demo.shape[0] // (rows_axis * cols_axis)
        plan = Plan(rows_axis, cols_axis, blk, demo.shape[1])
        return jax.shard_map(
            functools.partial(body, plan),
            mesh=mesh,
            in_specs=(P(("row", "col"), None), P(("row", "col"), None)),
            out_specs=(P(("row", "col")), P(("row", "col")), P(("row", "col"))),
            check_vma=False,
        )(demo, rollout)

    return run
```

```python
import functools
import math

import jax
import jax.numpy as jnp
from jax import lax
from jax.experimental import pallas as pl
from jax.experimental.pallas import tpu as pltpu
from jax.sharding import PartitionSpec as P

EPS = 0.005
MESH = pl.DeviceIdType.MESH
LANES = 128
SUB = 8


class Plan:
    def __init__(self, rows_axis, cols_axis, blk, width):
        self.core = 2
        depth = rows_axis // 2
        self.x = 1 << ((cols_axis.bit_length() - 1) // 2)
        self.y = cols_axis // self.x
        self.zl = min(depth, max(1, cols_axis // self.x))
        self.zh = depth // self.zl
        self.blk = blk
        self.width = width
        self.gr = self.zl * self.x
        self.gc = self.zh * self.y * self.core
        self.rows = self.gr * blk
        self.cols = self.gc * blk
        self.total = rows_axis * cols_axis * blk
        self.pieces = max(1, min(4, blk // 16))
        self.piece = blk // self.pieces
        self.chunks = 2 if blk % LANES == 0 and self.gr % 2 == 0 else 1


def normalize(embed):
    values = embed.astype(jnp.float32)
    inverse = lax.rsqrt(jnp.sum(values * values, axis=-1, keepdims=True) + 1e-06)
    return (values * inverse).astype(jnp.bfloat16)


def tree(op, items):
    items = list(items)
    while len(items) > 1:
        items = [
            op(items[i], items[i + 1]) if i + 1 < len(items) else items[i]
            for i in range(0, len(items), 2)
        ]
    return items[0]


def kernel(
    plan,
    demo_hbm,
    roll_hbm,
    out_ref,
    demo_ref,
    roll_ref,
    dem,
    rol,
    dist,
    kern,
    best,
    part,
    wide,
    scale,
    lf1,
    lf2,
    lg,
    f_all,
    g_all,
    cw_out,
    cw_in,
    s_in,
    s_dem,
    r_dem,
    s_rol,
    r_rol,
    s_f1,
    r_f1,
    s_f2,
    r_f2,
    s_g,
    r_g,
    s_c,
    r_c,
):
    blk, rows, cols = plan.blk, plan.rows, plan.cols
    n_parts = cols // LANES
    chunks, chunk = plan.chunks, rows // plan.chunks
    row = lax.axis_index("row")
    col = lax.axis_index("col")
    core, z = lax.rem(row, 2), row // 2
    zlo, zhi = lax.rem(z, plan.zl), z // plan.zl
    x, y = lax.rem(col, plan.x), col // plan.x

    load_demo = pltpu.make_async_copy(demo_hbm, demo_ref, s_in.at[0])
    load_roll = pltpu.make_async_copy(roll_hbm, roll_ref, s_in.at[1])
    load_demo.start()
    load_roll.start()

    def row_peer(dz, dx):
        zz, xx = lax.rem(zlo + dz, plan.zl), lax.rem(x + dx, plan.x)
        device = ((zhi * plan.zl + zz) * 2 + core, y * plan.x + xx)
        return device, zz * plan.x + xx

    def col_peer(dz, dy, dc):
        zz, yy, cc = lax.rem(zhi + dz, plan.zh), lax.rem(y + dy, plan.y), lax.rem(core + dc, 2)
        device = ((zz * plan.zl + zlo) * 2 + cc, yy * plan.x + x)
        return device, (zz * plan.y + yy) * 2 + cc

    row_offsets = [(a, b) for a in range(plan.zl) for b in range(plan.x)]
    col_offsets = [(a, b, c) for a in range(plan.zh) for b in range(plan.y) for c in range(2)]
    row_peers = {o: row_peer(*o) for o in row_offsets}
    col_peers = {o: col_peer(*o) for o in col_offsets}
    p_me = row_peers[(0, 0)][1]
    q_me = col_peers[(0, 0, 0)][1]
    row_others = [row_peers[o] for o in row_offsets[1:]]
    col_others = [col_peers[o] for o in col_offsets[1:]]
    places = [col_peers[o][1] for o in col_offsets]

    barrier = pltpu.get_barrier_semaphore()
    for device, _ in row_others + col_others:
        pl.semaphore_signal(barrier, inc=1, device_id=device, device_id_type=MESH)

    def slot(buf, index, piece):
        start = pl.multiple_of(index * blk + piece * plan.piece, 16)
        return buf.at[pl.ds(start, plan.piece), :]

    load_demo.wait()
    dem[pl.ds(pl.multiple_of(p_me * blk, 16), blk), :] = normalize(demo_ref[...])
    load_roll.wait()
    rol[pl.ds(pl.multiple_of(q_me * blk, 16), blk), :] = normalize(roll_ref[...])
    pl.semaphore_wait(barrier, len(row_others) + len(col_others))

    partner = col_peers[(0, 0, 1)][0]
    started = []

    def send(buf, index, piece, device, ssem, rsem, count):
        ref = slot(buf, index, piece)
        copy = pltpu.make_async_remote_copy(
            src_ref=ref,
            dst_ref=ref,
            send_sem=ssem.at[count[0]],
            recv_sem=rsem.at[index, piece],
            device_id=device,
            device_id_type=MESH,
        )
        copy.start()
        count[0] += 1
        started.append(copy)

    def arrived(buf, index, piece, ssem, rsem):
        ref = slot(buf, index, piece)
        pltpu.make_async_remote_copy(
            src_ref=ref,
            dst_ref=ref,
            send_sem=ssem.at[0],
            recv_sem=rsem.at[index, piece],
            device_id=partner,
            device_id_type=MESH,
        ).wait_recv()

    n_dem, n_rol = [0], [0]
    send_dem = lambda i, k, d: send(dem, i, k, d, s_dem, r_dem, n_dem)
    send_rol = lambda i, k, d: send(rol, i, k, d, s_rol, r_rol, n_rol)
    for k in range(plan.pieces):
        for dz in range(1, plan.zl):
            send_dem(p_me, k, row_peers[(dz, 0)][0])
        for dz in range(1, plan.zh):
            send_rol(q_me, k, col_peers[(dz, 0, 0)][0])
        for dx in range(1, plan.x):
            send_dem(p_me, k, row_peers[(0, dx)][0])
        for dy in range(1, plan.y):
            send_rol(q_me, k, col_peers[(0, dy, 0)][0])
        send_rol(q_me, k, partner)
    for k in range(plan.pieces):
        for dz in range(1, plan.zl):
            index = row_peers[(dz, 0)][1]
            arrived(dem, index, k, s_dem, r_dem)
            for dx in range(1, plan.x):
                send_dem(index, k, row_peers[(0, dx)][0])
        for dz in range(1, plan.zh):
            index = col_peers[(dz, 0, 0)][1]
            arrived(rol, index, k, s_rol, r_rol)
            for dy in range(1, plan.y):
                send_rol(index, k, col_peers[(0, dy, 0)][0])
            send_rol(index, k, partner)
        for dy in range(1, plan.y):
            index = col_peers[(0, dy, 0)][1]
            arrived(rol, index, k, s_rol, r_rol)
            send_rol(index, k, partner)
    for k in range(plan.pieces):
        for dz in range(plan.zl):
            for dx in range(1, plan.x):
                arrived(dem, row_peers[(dz, dx)][1], k, s_dem, r_dem)

    def lanes(c):
        return slice(c * LANES, (c + 1) * LANES)

    def group(r):
        return pl.ds(pl.multiple_of(r * SUB, SUB), SUB)

    def over(h, body, init, unroll):
        first = h * chunk // SUB
        return lax.fori_loop(first, first + chunk // SUB, body, init, unroll=unroll)

    eye = lax.broadcasted_iota(jnp.int32, (LANES, LANES), 0) == lax.broadcasted_iota(
        jnp.int32, (LANES, LANES), 1
    )

    def to_lanes(column):
        return jnp.sum(jnp.where(eye, column, 0.0), axis=0, keepdims=True)

    def tile(where, count):
        for i in range(where, where + count):
            inner = lax.dot_general(
                dem[...],
                rol[pl.ds(pl.multiple_of(places[i] * blk, 16), blk), :],
                (((1,), (1,)), ((), ())),
                preferred_element_type=jnp.float32,
            )
            dist[:, i * blk : (i + 1) * blk] = (1.0 - inner) * (1.0 / EPS)

    def row_stats(h, first, count, fresh):
        def step(r, carry):
            here = group(r)
            values = [dist[here, lanes(c)] for c in range(first, first + count)]
            low = tree(jnp.minimum, values)
            if not fresh:
                before = best[here, :]
                low = jnp.minimum(low, before)
            total = tree(jnp.add, [jnp.exp(low - v) for v in values])
            if not fresh:
                total = total + part[here, :] * jnp.exp(low - before)
            best[here, :] = low
            part[here, :] = total
            return carry

        over(h, step, 0, max(4, 64 // count))

    def store_line(buf, index, k, line):
        at = k * LANES
        done = 0
        while done < LANES:
            i, j = (at + done) // blk, (at + done) % blk
            n = min(LANES - done, blk - j)
            buf[index, i : i + 1, j : j + n] = line[:, done : done + n]
            done += n

    def exchange_start(buf, index, others, ssem, rsem, h, slots):
        here = pl.ds(h * slots, slots)
        for i, (device, _) in enumerate(others):
            copy = pltpu.make_async_remote_copy(
                src_ref=buf.at[index, here],
                dst_ref=buf.at[index, here],
                send_sem=ssem.at[i, h],
                recv_sem=rsem.at[index, h],
                device_id=device,
                device_id_type=MESH,
            )
            copy.start()
            started.append(copy)

    def exchange_wait(buf, others, ssem, rsem, h, slots):
        here = pl.ds(h * slots, slots)
        for i, (device, other) in enumerate(others):
            pltpu.make_async_remote_copy(
                src_ref=buf.at[other, here],
                dst_ref=buf.at[other, here],
                send_sem=ssem.at[i, h],
                recv_sem=rsem.at[other, h],
                device_id=device,
                device_id_type=MESH,
            ).wait_recv()

    def log_total(values):
        top = tree(jnp.maximum, values)
        return top + jnp.log(tree(jnp.add, [jnp.exp(v - top) for v in values]))

    def line_of(pieces):
        return pieces[0] if len(pieces) == 1 else jnp.concatenate(pieces, axis=1)

    def spread(h, values):
        line = line_of([values[i : i + 1, :] for i in range(values.shape[0])])
        for k in range(chunk // LANES):
            column = jnp.sum(jnp.where(eye, line[:, lanes(k)], 0.0), axis=1, keepdims=True)
            wide[lanes(h * (chunk // LANES) + k), :] = jnp.broadcast_to(column, (LANES, LANES))

    per_chunk = chunk // LANES
    slots = chunk // blk
    log_n = math.log(plan.total)

    every = [o for o in col_offsets if o[2] == 0]
    fresh = True
    done = 0
    for at, (dz, dy, _) in enumerate(every):
        if dz > 0 and dy > 0:
            for k in range(plan.pieces):
                index = col_peers[(dz, dy, 0)][1]
                arrived(rol, index, k, s_rol, r_rol)
                send_rol(index, k, partner)
        for k in range(plan.pieces):
            arrived(rol, col_peers[(dz, dy, 1)][1], k, s_rol, r_rol)
        tile(2 * at, 2)
        if (2 * (at + 1) * blk) % LANES == 0 and at + 1 < len(every):
            upto = 2 * (at + 1) * blk // LANES
            for h in range(chunks):
                row_stats(h, done, upto - done, fresh)
            fresh, done = False, upto
    for h in range(chunks):
        row_stats(h, done, n_parts - done, fresh)
        for k in range(h * per_chunk, (h + 1) * per_chunk):
            low = best[lanes(k), :]
            least = jnp.min(low, axis=1, keepdims=True)
            total = jnp.sum(part[lanes(k), :] * jnp.exp(least - low), axis=1, keepdims=True)
            store_line(lf1, p_me, k, jnp.log(to_lanes(total)) - to_lanes(least))
        exchange_start(lf1, p_me, row_others, s_f1, r_f1, h, slots)

    def col_max(r, carry):
        here = group(r)
        f_here = wide[here, :]
        return tuple(
            jnp.maximum(carry[c], f_here - dist[here, lanes(c)]) for c in range(n_parts)
        )

    tops = tuple(jnp.full((SUB, LANES), -jnp.inf, jnp.float32) for _ in range(n_parts))
    for h in range(chunks):
        exchange_wait(lf1, row_others, s_f1, r_f1, h, slots)
        here = pl.ds(h * slots, slots)
        f_all[here, :] = -log_n - log_total([lf1[i, here, :] for i in range(plan.gr)])
        spread(h, f_all[here, :])
        tops = over(h, col_max, tops, 8)

    def col_sum(r, carry):
        here = group(r)
        f_here = wide[here, :]
        out = []
        for c in range(n_parts):
            value = jnp.exp((f_here - dist[here, lanes(c)]) - tops[c])
            kern[here, lanes(c)] = value
            out.append(carry[c] + value)
        return tuple(out)

    zeros = tuple(jnp.zeros((SUB, LANES), jnp.float32) for _ in range(n_parts))
    sums = lax.fori_loop(0, rows // SUB, col_sum, zeros, unroll=8)
    pieces = []
    for c in range(n_parts):
        top = jnp.max(tops[c], axis=0, keepdims=True)
        total = jnp.sum(sums[c] * jnp.exp(tops[c] - top), axis=0, keepdims=True)
        pieces.append(top + jnp.log(total))
    line = line_of(pieces)
    for i, place in enumerate(places):
        lg[q_me, pl.ds(place, 1), :] = line[:, i * blk : (i + 1) * blk]
    exchange_start(lg, q_me, col_others, s_g, r_g, 0, plan.gc)
    exchange_wait(lg, col_others, s_g, r_g, 0, plan.gc)
    g_all[...] = -log_n - log_total([lg[i] for i in range(plan.gc)])
    g_line = line_of([g_all[pl.ds(place, 1), :] for place in places])
    for c in range(n_parts):
        scale[:, lanes(c)] = jnp.exp(tops[c] + g_line[:, lanes(c)])

    def second_rows(r, carry):
        here = group(r)
        part[here, :] = tree(
            jnp.add, [kern[here, lanes(c)] * scale[:, lanes(c)] for c in range(n_parts)]
        )
        return carry

    for h in range(chunks):
        over(h, second_rows, 0, 8)
        for k in range(h * per_chunk, (h + 1) * per_chunk):
            total = jnp.sum(part[lanes(k), :], axis=1, keepdims=True)
            store_line(lf2, p_me, k, to_lanes(total))
        exchange_start(lf2, p_me, row_others, s_f2, r_f2, h, slots)

    def last(r, carry):
        here = group(r)
        u_here = wide[here, :]
        mass_c, cost_c = carry
        new_mass, new_cost = [], []
        for c in range(n_parts):
            value = u_here * kern[here, lanes(c)]
            new_mass.append(mass_c[c] + value)
            new_cost.append(cost_c[c] + value * dist[here, lanes(c)])
        return tuple(new_mass), tuple(new_cost)

    both = (zeros, zeros)
    for h in range(chunks):
        exchange_wait(lf2, row_others, s_f2, r_f2, h, slots)
        here = pl.ds(h * slots, slots)
        mass = tree(jnp.add, [lf2[i, here, :] for i in range(plan.gr)]) * float(plan.total)
        spread(h, 1.0 / mass)
        f_all[here, :] = f_all[here, :] - jnp.log(mass)
        both = over(h, last, both, 4)

    def finish(values):
        return line_of(
            [
                jnp.sum(values[c] * scale[:, lanes(c)], axis=0, keepdims=True)
                for c in range(n_parts)
            ]
        )

    both = jnp.concatenate([finish(both[0]), finish(both[1])], axis=0)
    for i, place in enumerate(places):
        cw_out[place] = both[:, i * blk : (i + 1) * blk]
    for i, (device, other) in enumerate(col_others):
        copy = pltpu.make_async_remote_copy(
            src_ref=cw_out.at[other],
            dst_ref=cw_in.at[q_me],
            send_sem=s_c.at[i],
            recv_sem=r_c.at[q_me],
            device_id=device,
            device_id_type=MESH,
        )
        copy.start()
        started.append(copy)
    cw_in[q_me] = cw_out[q_me]
    for i, (device, other) in enumerate(col_others):
        pltpu.make_async_remote_copy(
            src_ref=cw_out.at[other],
            dst_ref=cw_in.at[other],
            send_sem=s_c.at[i],
            recv_sem=r_c.at[other],
            device_id=device,
            device_id_type=MESH,
        ).wait_recv()
    total = tree(jnp.add, [cw_in[i] for i in range(plan.gc)])
    out_ref[0:1, :] = f_all[pl.ds(p_me, 1), :]
    out_ref[1:2, :] = g_all[pl.ds(q_me, 1), :] - jnp.log(total[0:1] * float(plan.total))
    out_ref[2:3, :] = total[1:2] / total[0:1] * -EPS
    for copy in started:
        copy.wait_send()


def body(plan, demo, rollout):
    blk, width, rows, cols = plan.blk, plan.width, plan.rows, plan.cols
    n_dem = plan.pieces * ((plan.zl - 1) + (plan.x - 1) * plan.zl)
    n_rol = plan.pieces * (
        (plan.zh - 1) + (plan.y - 1) * plan.zh + plan.zh * plan.y
    )
    dma = pltpu.SemaphoreType.DMA
    f32 = jnp.float32
    out = pl.pallas_call(
        functools.partial(kernel, plan),
        out_shape=jax.ShapeDtypeStruct((3, blk), f32),
        in_specs=[pl.BlockSpec(memory_space=pltpu.HBM)] * 2,
        out_specs=pl.BlockSpec(memory_space=pltpu.VMEM),
        scratch_shapes=[
            pltpu.VMEM((blk, width), jnp.bfloat16),
            pltpu.VMEM((blk, width), jnp.bfloat16),
            pltpu.VMEM((rows, width), jnp.bfloat16),
            pltpu.VMEM((cols, width), jnp.bfloat16),
            pltpu.VMEM((rows, cols), f32),
            pltpu.VMEM((rows, cols), f32),
            pltpu.VMEM((rows, LANES), f32),
            pltpu.VMEM((rows, LANES), f32),
            pltpu.VMEM((rows, LANES), f32),
            pltpu.VMEM((SUB, cols), f32),
            pltpu.VMEM((plan.gr, plan.gr, blk), f32),
            pltpu.VMEM((plan.gr, plan.gr, blk), f32),
            pltpu.VMEM((plan.gc, plan.gc, blk), f32),
            pltpu.VMEM((plan.gr, blk), f32),
            pltpu.VMEM((plan.gc, blk), f32),
            pltpu.VMEM((plan.gc, 2, blk), f32),
            pltpu.VMEM((plan.gc, 2, blk), f32),
            dma((2,)),
            dma((n_dem,)),
            dma((plan.gr, plan.pieces)),
            dma((n_rol,)),
            dma((plan.gc, plan.pieces)),
            dma((plan.gr, plan.chunks)),
            dma((plan.gr, plan.chunks)),
            dma((plan.gr, plan.chunks)),
            dma((plan.gr, plan.chunks)),
            dma((plan.gc, 1)),
            dma((plan.gc, 1)),
            dma((plan.gc,)),
            dma((plan.gc,)),
        ],
        compiler_params=pltpu.CompilerParams(
            collective_id=0, has_side_effects=True, vmem_limit_bytes=64 * 1024 * 1024 - 128 * 1024
        ),
    )(demo, rollout)
    return out[0], out[1], out[2]


def solution(mesh):
    rows_axis, cols_axis = mesh.shape["row"], mesh.shape["col"]

    def run(demo, rollout):
        blk = demo.shape[0] // (rows_axis * cols_axis)
        plan = Plan(rows_axis, cols_axis, blk, demo.shape[1])
        return jax.shard_map(
            functools.partial(body, plan),
            mesh=mesh,
            in_specs=(P(("row", "col"), None), P(("row", "col"), None)),
            out_specs=(P(("row", "col")), P(("row", "col")), P(("row", "col"))),
            check_vma=False,
        )(demo, rollout)

    return run
```

```python
import functools
import math

import jax
import jax.numpy as jnp
from jax import lax
from jax.experimental import pallas as pl
from jax.experimental.pallas import tpu as pltpu
from jax.sharding import PartitionSpec as P

EPS = 0.005
MESH = pl.DeviceIdType.MESH
LANES = 128
SUB = 8
GROUPS = 8
BLOCK = SUB * GROUPS


class Plan:
    def __init__(self, rows_axis, cols_axis, blk, width):
        self.core = 2
        depth = rows_axis // 2
        self.x = 1 << ((cols_axis.bit_length() - 1) // 2)
        self.y = cols_axis // self.x
        self.zl = min(depth, max(1, cols_axis // self.x))
        self.zh = depth // self.zl
        self.blk = blk
        self.width = width
        self.gr = self.zl * self.x
        self.gc = self.zh * self.y * self.core
        self.rows = self.gr * blk
        self.cols = self.gc * blk
        self.total = rows_axis * cols_axis * blk
        self.pieces = max(1, min(4, blk // 16))
        self.piece = blk // self.pieces
        self.fine = blk % LANES == 0 and (self.zl, self.x, self.zh, self.y, self.pieces) == (2, 2, 2, 2, 4)
        self.chunks = 2 if blk % LANES == 0 and self.gr % 2 == 0 else 1


def normalize(embed):
    values = embed.astype(jnp.float32)
    inverse = lax.rsqrt(jnp.sum(values * values, axis=-1, keepdims=True) + 1e-06)
    return (values * inverse).astype(jnp.bfloat16)


def tree(op, items):
    items = list(items)
    while len(items) > 1:
        items = [
            op(items[i], items[i + 1]) if i + 1 < len(items) else items[i]
            for i in range(0, len(items), 2)
        ]
    return items[0]


def kernel(
    plan,
    demo_hbm,
    roll_hbm,
    out_ref,
    demo_ref,
    roll_ref,
    dem,
    rol,
    dist,
    kern,
    best,
    part,
    wide,
    tops,
    sums,
    mass_c,
    cost_c,
    lf1,
    lf2,
    lg,
    f_all,
    g_all,
    cw_out,
    cw_in,
    s_in,
    s_dem,
    r_dem,
    s_rol,
    r_rol,
    s_f1,
    r_f1,
    s_f2,
    r_f2,
    s_g,
    r_g,
    s_c,
    r_c,
):
    blk, rows, cols = plan.blk, plan.rows, plan.cols
    n_parts = cols // LANES
    chunks, chunk = plan.chunks, rows // plan.chunks
    row = lax.axis_index("row")
    col = lax.axis_index("col")
    core, z = lax.rem(row, 2), row // 2
    zlo, zhi = lax.rem(z, plan.zl), z // plan.zl
    x, y = lax.rem(col, plan.x), col // plan.x

    load_demo = pltpu.make_async_copy(demo_hbm, demo_ref, s_in.at[0])
    load_roll = pltpu.make_async_copy(roll_hbm, roll_ref, s_in.at[1])
    load_demo.start()
    load_roll.start()

    def row_peer(dz, dx):
        zz, xx = lax.rem(zlo + dz, plan.zl), lax.rem(x + dx, plan.x)
        device = ((zhi * plan.zl + zz) * 2 + core, y * plan.x + xx)
        return device, zz * plan.x + xx

    def col_peer(dz, dy, dc):
        zz, yy, cc = lax.rem(zhi + dz, plan.zh), lax.rem(y + dy, plan.y), lax.rem(core + dc, 2)
        device = ((zz * plan.zl + zlo) * 2 + cc, yy * plan.x + x)
        return device, (zz * plan.y + yy) * 2 + cc

    row_offsets = [(a, b) for a in range(plan.zl) for b in range(plan.x)]
    col_offsets = [(a, b, c) for a in range(plan.zh) for b in range(plan.y) for c in range(2)]
    row_peers = {o: row_peer(*o) for o in row_offsets}
    col_peers = {o: col_peer(*o) for o in col_offsets}
    p_me = row_peers[(0, 0)][1]
    q_me = col_peers[(0, 0, 0)][1]
    row_others = [row_peers[o] for o in row_offsets[1:]]
    col_others = [col_peers[o] for o in col_offsets[1:]]
    places = [col_peers[o][1] for o in col_offsets]

    barrier = pltpu.get_barrier_semaphore()
    for device, _ in row_others + col_others:
        pl.semaphore_signal(barrier, inc=1, device_id=device, device_id_type=MESH)

    def slot(buf, index, piece):
        start = pl.multiple_of(index * blk + piece * plan.piece, 16)
        return buf.at[pl.ds(start, plan.piece), :]

    load_demo.wait()
    dem[pl.ds(pl.multiple_of(p_me * blk, 16), blk), :] = normalize(demo_ref[...])
    load_roll.wait()
    rol[pl.ds(pl.multiple_of(q_me * blk, 16), blk), :] = normalize(roll_ref[...])
    pl.semaphore_wait(barrier, len(row_others) + len(col_others))

    partner = col_peers[(0, 0, 1)][0]
    started = []

    def send(buf, index, piece, device, ssem, rsem, count):
        ref = slot(buf, index, piece)
        copy = pltpu.make_async_remote_copy(
            src_ref=ref,
            dst_ref=ref,
            send_sem=ssem.at[count[0]],
            recv_sem=rsem.at[index, piece],
            device_id=device,
            device_id_type=MESH,
        )
        copy.start()
        count[0] += 1
        started.append(copy)

    def arrived(buf, index, piece, ssem, rsem):
        ref = slot(buf, index, piece)
        pltpu.make_async_remote_copy(
            src_ref=ref,
            dst_ref=ref,
            send_sem=ssem.at[0],
            recv_sem=rsem.at[index, piece],
            device_id=partner,
            device_id_type=MESH,
        ).wait_recv()

    n_dem, n_rol = [0], [0]
    send_dem = lambda i, k, d: send(dem, i, k, d, s_dem, r_dem, n_dem)
    send_rol = lambda i, k, d: send(rol, i, k, d, s_rol, r_rol, n_rol)
    for k in range(plan.pieces):
        for dz in range(1, plan.zl):
            send_dem(p_me, k, row_peers[(dz, 0)][0])
        for dz in range(1, plan.zh):
            send_rol(q_me, k, col_peers[(dz, 0, 0)][0])
        for dx in range(1, plan.x):
            send_dem(p_me, k, row_peers[(0, dx)][0])
        for dy in range(1, plan.y):
            send_rol(q_me, k, col_peers[(0, dy, 0)][0])
        send_rol(q_me, k, partner)
    def lanes(c):
        return slice(c * LANES, (c + 1) * LANES)

    def group(r):
        return pl.ds(pl.multiple_of(r * SUB, SUB), SUB)

    def over(h, body, init, unroll):
        first = h * chunk // BLOCK
        return lax.fori_loop(first, first + chunk // BLOCK, body, init, unroll=unroll)

    eye = lax.broadcasted_iota(jnp.int32, (LANES, LANES), 0) == lax.broadcasted_iota(
        jnp.int32, (LANES, LANES), 1
    )

    def to_lanes(column):
        return jnp.sum(jnp.where(eye, column, 0.0), axis=0, keepdims=True)

    def tile(where, place):
        first = 0 if where is None else pl.multiple_of(where * blk, 16)
        here = pl.ds(first, rows if where is None else blk)
        for i in range(2 * place, 2 * place + 2):
            inner = lax.dot_general(
                dem[here, :],
                rol[pl.ds(pl.multiple_of(places[i] * blk, 16), blk), :],
                (((1,), (1,)), ((), ())),
                preferred_element_type=jnp.float32,
            )
            dist[here, i * blk : (i + 1) * blk] = (1.0 - inner) * (1.0 / EPS)

    def row_stats(first_row, size, place):
        pair = 2 * blk // LANES

        def step(r, carry):
            here = pl.ds(pl.multiple_of(first_row + r * SUB, SUB), SUB)
            values = [dist[here, lanes(c)] for c in range(place * pair, (place + 1) * pair)]
            low = tree(jnp.minimum, values)
            if place > 0:
                before = best[here, :]
                low = jnp.minimum(low, before)
            total = tree(jnp.add, [jnp.exp(low - v) for v in values])
            if place > 0:
                total = total + part[here, :] * jnp.exp(low - before)
            best[here, :] = low
            part[here, :] = total
            return carry

        lax.fori_loop(0, size // SUB, step, 0, unroll=16)

    def unit(where, place):
        tile(where, place)
        row_stats(pl.multiple_of(where * blk, SUB), blk, place)

    def store_line(buf, index, k, line):
        at = k * LANES
        done = 0
        while done < LANES:
            i, j = (at + done) // blk, (at + done) % blk
            n = min(LANES - done, blk - j)
            buf[index, i : i + 1, j : j + n] = line[:, done : done + n]
            done += n

    def exchange_start(buf, index, others, ssem, rsem, h, slots):
        here = pl.ds(h * slots, slots)
        for i, (device, _) in enumerate(others):
            copy = pltpu.make_async_remote_copy(
                src_ref=buf.at[index, here],
                dst_ref=buf.at[index, here],
                send_sem=ssem.at[i, h],
                recv_sem=rsem.at[index, h],
                device_id=device,
                device_id_type=MESH,
            )
            copy.start()
            started.append(copy)

    def exchange_wait(buf, others, ssem, rsem, h, slots):
        here = pl.ds(h * slots, slots)
        for i, (device, other) in enumerate(others):
            pltpu.make_async_remote_copy(
                src_ref=buf.at[other, here],
                dst_ref=buf.at[other, here],
                send_sem=ssem.at[i, h],
                recv_sem=rsem.at[other, h],
                device_id=device,
                device_id_type=MESH,
            ).wait_recv()

    def log_total(values):
        top = tree(jnp.maximum, values)
        return top + jnp.log(tree(jnp.add, [jnp.exp(v - top) for v in values]))

    def line_of(pieces):
        return pieces[0] if len(pieces) == 1 else jnp.concatenate(pieces, axis=1)

    def spread(h, values):
        line = line_of([values[i : i + 1, :] for i in range(values.shape[0])])
        for k in range(chunk // LANES):
            column = jnp.sum(jnp.where(eye, line[:, lanes(k)], 0.0), axis=1, keepdims=True)
            wide[lanes(h * (chunk // LANES) + k), :] = jnp.broadcast_to(column, (LANES, LANES))

    per_chunk = chunk // LANES
    slots = chunk // blk
    log_n = math.log(plan.total)

    def forward(k):
        for dz in range(1, plan.zl):
            index = row_peers[(dz, 0)][1]
            arrived(dem, index, k, s_dem, r_dem)
            for dx in range(1, plan.x):
                send_dem(index, k, row_peers[(0, dx)][0])
        for dz in range(1, plan.zh):
            index = col_peers[(dz, 0, 0)][1]
            arrived(rol, index, k, s_rol, r_rol)
            for dy in range(1, plan.y):
                send_rol(index, k, col_peers[(0, dy, 0)][0])
            send_rol(index, k, partner)
        for dy in range(1, plan.y):
            index = col_peers[(0, dy, 0)][1]
            arrived(rol, index, k, s_rol, r_rol)
            send_rol(index, k, partner)

    def relay():
        for k in range(plan.pieces):
            for dz in range(1, plan.zh):
                for dy in range(1, plan.y):
                    index = col_peers[(dz, dy, 0)][1]
                    arrived(rol, index, k, s_rol, r_rol)
                    send_rol(index, k, partner)

    def rows_in(dz, dx):
        index = row_peers[(dz, dx)][1]
        for k in range(plan.pieces):
            arrived(dem, index, k, s_dem, r_dem)
        return index

    def cols_in(dz, dy):
        for k in range(plan.pieces):
            arrived(rol, col_peers[(dz, dy, 1)][1], k, s_rol, r_rol)

    if plan.fine:
        own, near_y, near_z, far = range(4)
        cols_in(0, 0)
        unit(p_me, own)
        forward(0)
        forward(1)
        row_x = rows_in(0, 1)
        unit(row_x, own)
        forward(2)
        forward(3)
        row_z = row_peers[(1, 0)][1]
        cols_in(0, 1)
        unit(p_me, near_y)
        unit(row_z, own)
        relay()
        unit(row_x, near_y)
        unit(row_z, near_y)
        cols_in(1, 0)
        for index in (p_me, row_x, row_z):
            unit(index, near_z)
        row_f = rows_in(1, 1)
        for place in (own, near_y, near_z):
            unit(row_f, place)
        cols_in(1, 1)
        tile(None, far)
        last_place = far
    else:
        for k in range(plan.pieces):
            forward(k)
        relay()
        for dz in range(plan.zl):
            for dx in range(1, plan.x):
                rows_in(dz, dx)
        last_place = len(places) // 2 - 1
        for place in range(last_place + 1):
            cols_in(*col_offsets[2 * place][:2])
            tile(None, place)
            if place < last_place:
                row_stats(0, rows, place)

    for h in range(chunks):
        row_stats(h * chunk, chunk, last_place)
        for k in range(h * per_chunk, (h + 1) * per_chunk):
            low = best[lanes(k), :]
            least = jnp.min(low, axis=1, keepdims=True)
            total = jnp.sum(part[lanes(k), :] * jnp.exp(least - low), axis=1, keepdims=True)
            store_line(lf1, p_me, k, jnp.log(to_lanes(total)) - to_lanes(least))
        exchange_start(lf1, p_me, row_others, s_f1, r_f1, h, slots)

    def inside(b, g):
        return pl.ds(pl.multiple_of(b * BLOCK + g * SUB, SUB), SUB)

    def col_sum(b, carry):
        f_here = [wide[inside(b, g), :] for g in range(GROUPS)]
        for c in range(n_parts):
            values = [f_here[g] - dist[inside(b, g), lanes(c)] for g in range(GROUPS)]
            top = tree(jnp.maximum, values)
            values = [jnp.exp(v - top) for v in values]
            for g in range(GROUPS):
                kern[inside(b, g), lanes(c)] = values[g]
            tops[group(b), lanes(c)] = top
            sums[group(b), lanes(c)] = tree(jnp.add, values)
        return carry

    for h in range(chunks):
        exchange_wait(lf1, row_others, s_f1, r_f1, h, slots)
        here = pl.ds(h * slots, slots)
        f_all[here, :] = -log_n - log_total([lf1[i, here, :] for i in range(plan.gr)])
        spread(h, f_all[here, :])
        over(h, col_sum, 0, 1)

    blocks = rows // BLOCK
    pieces = []
    for c in range(n_parts):
        top = tree(jnp.maximum, [tops[b * SUB : (b + 1) * SUB, lanes(c)] for b in range(blocks)])
        top = jnp.max(top, axis=0, keepdims=True)
        total = tree(
            jnp.add,
            [
                sums[b * SUB : (b + 1) * SUB, lanes(c)]
                * jnp.exp(tops[b * SUB : (b + 1) * SUB, lanes(c)] - top)
                for b in range(blocks)
            ],
        )
        pieces.append(top + jnp.log(jnp.sum(total, axis=0, keepdims=True)))
    line = line_of(pieces)
    for i, place in enumerate(places):
        lg[q_me, pl.ds(place, 1), :] = line[:, i * blk : (i + 1) * blk]
    exchange_start(lg, q_me, col_others, s_g, r_g, 0, plan.gc)
    exchange_wait(lg, col_others, s_g, r_g, 0, plan.gc)
    g_all[...] = -log_n - log_total([lg[i] for i in range(plan.gc)])
    g_line = line_of([g_all[pl.ds(place, 1), :] for place in places])
    for c in range(n_parts):
        tops[:, lanes(c)] = jnp.exp(tops[:, lanes(c)] + g_line[:, lanes(c)])

    def second_rows(b, carry):
        totals = [None] * GROUPS
        for c in range(n_parts):
            scale = tops[group(b), lanes(c)]
            for g in range(GROUPS):
                value = kern[inside(b, g), lanes(c)] * scale
                totals[g] = value if c == 0 else totals[g] + value
        for g in range(GROUPS):
            part[inside(b, g), :] = totals[g]
        return carry

    for h in range(chunks):
        over(h, second_rows, 0, 1)
        for k in range(h * per_chunk, (h + 1) * per_chunk):
            total = jnp.sum(part[lanes(k), :], axis=1, keepdims=True)
            store_line(lf2, p_me, k, to_lanes(total))
        exchange_start(lf2, p_me, row_others, s_f2, r_f2, h, slots)

    def last(b, carry):
        u_here = [wide[inside(b, g), :] for g in range(GROUPS)]
        for c in range(n_parts):
            scale = tops[group(b), lanes(c)]
            values = [u_here[g] * kern[inside(b, g), lanes(c)] for g in range(GROUPS)]
            mass_c[:, lanes(c)] += tree(jnp.add, values) * scale
            values = [values[g] * dist[inside(b, g), lanes(c)] for g in range(GROUPS)]
            cost_c[:, lanes(c)] += tree(jnp.add, values) * scale
        return carry

    mass_c[...] = jnp.zeros_like(mass_c)
    cost_c[...] = jnp.zeros_like(cost_c)
    for h in range(chunks):
        exchange_wait(lf2, row_others, s_f2, r_f2, h, slots)
        here = pl.ds(h * slots, slots)
        mass = tree(jnp.add, [lf2[i, here, :] for i in range(plan.gr)]) * float(plan.total)
        spread(h, 1.0 / mass)
        f_all[here, :] = f_all[here, :] - jnp.log(mass)
        over(h, last, 0, 1)

    both = jnp.concatenate(
        [
            jnp.sum(mass_c[...], axis=0, keepdims=True),
            jnp.sum(cost_c[...], axis=0, keepdims=True),
        ],
        axis=0,
    )
    for i, place in enumerate(places):
        cw_out[place] = both[:, i * blk : (i + 1) * blk]
    for i, (device, other) in enumerate(col_others):
        copy = pltpu.make_async_remote_copy(
            src_ref=cw_out.at[other],
            dst_ref=cw_in.at[q_me],
            send_sem=s_c.at[i],
            recv_sem=r_c.at[q_me],
            device_id=device,
            device_id_type=MESH,
        )
        copy.start()
        started.append(copy)
    cw_in[q_me] = cw_out[q_me]
    for i, (device, other) in enumerate(col_others):
        pltpu.make_async_remote_copy(
            src_ref=cw_out.at[other],
            dst_ref=cw_in.at[other],
            send_sem=s_c.at[i],
            recv_sem=r_c.at[other],
            device_id=device,
            device_id_type=MESH,
        ).wait_recv()
    total = tree(jnp.add, [cw_in[i] for i in range(plan.gc)])
    out_ref[0:1, :] = f_all[pl.ds(p_me, 1), :]
    out_ref[1:2, :] = g_all[pl.ds(q_me, 1), :] - jnp.log(total[0:1] * float(plan.total))
    out_ref[2:3, :] = total[1:2] / total[0:1] * -EPS
    for copy in started:
        copy.wait_send()


def body(plan, demo, rollout):
    blk, width, rows, cols = plan.blk, plan.width, plan.rows, plan.cols
    n_dem = plan.pieces * ((plan.zl - 1) + (plan.x - 1) * plan.zl)
    n_rol = plan.pieces * (
        (plan.zh - 1) + (plan.y - 1) * plan.zh + plan.zh * plan.y
    )
    dma = pltpu.SemaphoreType.DMA
    f32 = jnp.float32
    out = pl.pallas_call(
        functools.partial(kernel, plan),
        out_shape=jax.ShapeDtypeStruct((3, blk), f32),
        in_specs=[pl.BlockSpec(memory_space=pltpu.HBM)] * 2,
        out_specs=pl.BlockSpec(memory_space=pltpu.VMEM),
        scratch_shapes=[
            pltpu.VMEM((blk, width), jnp.bfloat16),
            pltpu.VMEM((blk, width), jnp.bfloat16),
            pltpu.VMEM((rows, width), jnp.bfloat16),
            pltpu.VMEM((cols, width), jnp.bfloat16),
            pltpu.VMEM((rows, cols), f32),
            pltpu.VMEM((rows, cols), f32),
            pltpu.VMEM((rows, LANES), f32),
            pltpu.VMEM((rows, LANES), f32),
            pltpu.VMEM((rows, LANES), f32),
            pltpu.VMEM((rows // GROUPS, cols), f32),
            pltpu.VMEM((rows // GROUPS, cols), f32),
            pltpu.VMEM((SUB, cols), f32),
            pltpu.VMEM((SUB, cols), f32),
            pltpu.VMEM((plan.gr, plan.gr, blk), f32),
            pltpu.VMEM((plan.gr, plan.gr, blk), f32),
            pltpu.VMEM((plan.gc, plan.gc, blk), f32),
            pltpu.VMEM((plan.gr, blk), f32),
            pltpu.VMEM((plan.gc, blk), f32),
            pltpu.VMEM((plan.gc, 2, blk), f32),
            pltpu.VMEM((plan.gc, 2, blk), f32),
            dma((2,)),
            dma((n_dem,)),
            dma((plan.gr, plan.pieces)),
            dma((n_rol,)),
            dma((plan.gc, plan.pieces)),
            dma((plan.gr, plan.chunks)),
            dma((plan.gr, plan.chunks)),
            dma((plan.gr, plan.chunks)),
            dma((plan.gr, plan.chunks)),
            dma((plan.gc, 1)),
            dma((plan.gc, 1)),
            dma((plan.gc,)),
            dma((plan.gc,)),
        ],
        compiler_params=pltpu.CompilerParams(
            collective_id=0, has_side_effects=True, vmem_limit_bytes=64 * 1024 * 1024 - 128 * 1024
        ),
    )(demo, rollout)
    return out[0], out[1], out[2]


def solution(mesh):
    rows_axis, cols_axis = mesh.shape["row"], mesh.shape["col"]

    def run(demo, rollout):
        blk = demo.shape[0] // (rows_axis * cols_axis)
        plan = Plan(rows_axis, cols_axis, blk, demo.shape[1])
        return jax.shard_map(
            functools.partial(body, plan),
            mesh=mesh,
            in_specs=(P(("row", "col"), None), P(("row", "col"), None)),
            out_specs=(P(("row", "col")), P(("row", "col")), P(("row", "col"))),
            check_vma=False,
        )(demo, rollout)

    return run
```

```python
import functools
import math

import jax
import jax.numpy as jnp
from jax import lax
from jax.experimental import pallas as pl
from jax.experimental.pallas import tpu as pltpu
from jax.sharding import PartitionSpec as P

EPS = 0.005
MESH = pl.DeviceIdType.MESH
LANES = 128
SUB = 8
GROUPS = 8
BLOCK = SUB * GROUPS


class Plan:
    def __init__(self, rows_axis, cols_axis, blk, width):
        self.core = 2
        depth = rows_axis // 2
        self.x = 1 << ((cols_axis.bit_length() - 1) // 2)
        self.y = cols_axis // self.x
        self.zl = min(depth, max(1, cols_axis // self.x))
        self.zh = depth // self.zl
        self.blk = blk
        self.width = width
        self.gr = self.zl * self.x
        self.gc = self.zh * self.y * self.core
        self.rows = self.gr * blk
        self.cols = self.gc * blk
        self.total = rows_axis * cols_axis * blk
        self.pieces = max(1, min(4, blk // 16))
        self.piece = blk // self.pieces
        self.chunks = 2 if blk % LANES == 0 and self.gr % 2 == 0 else 1


def normalize(embed):
    values = embed.astype(jnp.float32)
    inverse = lax.rsqrt(jnp.sum(values * values, axis=-1, keepdims=True) + 1e-06)
    return (values * inverse).astype(jnp.bfloat16)


def tree(op, items):
    items = list(items)
    while len(items) > 1:
        items = [
            op(items[i], items[i + 1]) if i + 1 < len(items) else items[i]
            for i in range(0, len(items), 2)
        ]
    return items[0]


def kernel(
    plan,
    demo_hbm,
    roll_hbm,
    out_ref,
    demo_ref,
    roll_ref,
    dem,
    rol,
    dist,
    kern,
    best,
    part,
    wide,
    tops,
    sums,
    mass_c,
    cost_c,
    lf1,
    lf2,
    lg,
    f_all,
    g_all,
    cw_out,
    cw_in,
    s_in,
    s_dem,
    r_dem,
    s_rol,
    r_rol,
    s_f1,
    r_f1,
    s_f2,
    r_f2,
    s_g,
    r_g,
    s_c,
    r_c,
):
    blk, rows, cols = plan.blk, plan.rows, plan.cols
    n_parts = cols // LANES
    chunks, chunk = plan.chunks, rows // plan.chunks
    row = lax.axis_index("row")
    col = lax.axis_index("col")
    core, z = lax.rem(row, 2), row // 2
    zlo, zhi = lax.rem(z, plan.zl), z // plan.zl
    x, y = lax.rem(col, plan.x), col // plan.x

    load_demo = pltpu.make_async_copy(demo_hbm, demo_ref, s_in.at[0])
    load_roll = pltpu.make_async_copy(roll_hbm, roll_ref, s_in.at[1])
    load_demo.start()
    load_roll.start()

    def row_peer(dz, dx):
        zz, xx = lax.rem(zlo + dz, plan.zl), lax.rem(x + dx, plan.x)
        device = ((zhi * plan.zl + zz) * 2 + core, y * plan.x + xx)
        return device, zz * plan.x + xx

    def col_peer(dz, dy, dc):
        zz, yy, cc = lax.rem(zhi + dz, plan.zh), lax.rem(y + dy, plan.y), lax.rem(core + dc, 2)
        device = ((zz * plan.zl + zlo) * 2 + cc, yy * plan.x + x)
        return device, (zz * plan.y + yy) * 2 + cc

    row_offsets = [(a, b) for a in range(plan.zl) for b in range(plan.x)]
    col_offsets = [(a, b, c) for a in range(plan.zh) for b in range(plan.y) for c in range(2)]
    row_peers = {o: row_peer(*o) for o in row_offsets}
    col_peers = {o: col_peer(*o) for o in col_offsets}
    p_me = row_peers[(0, 0)][1]
    q_me = col_peers[(0, 0, 0)][1]
    row_others = [row_peers[o] for o in row_offsets[1:]]
    col_others = [col_peers[o] for o in col_offsets[1:]]
    places = [col_peers[o][1] for o in col_offsets]

    barrier = pltpu.get_barrier_semaphore()
    for device, _ in row_others + col_others:
        pl.semaphore_signal(barrier, inc=1, device_id=device, device_id_type=MESH)

    def slot(buf, index, piece):
        start = pl.multiple_of(index * blk + piece * plan.piece, 16)
        return buf.at[pl.ds(start, plan.piece), :]

    load_demo.wait()
    dem[pl.ds(pl.multiple_of(p_me * blk, 16), blk), :] = normalize(demo_ref[...])
    load_roll.wait()
    rol[pl.ds(pl.multiple_of(q_me * blk, 16), blk), :] = normalize(roll_ref[...])
    pl.semaphore_wait(barrier, len(row_others) + len(col_others))

    partner = col_peers[(0, 0, 1)][0]
    started = []
    per_dem = (plan.zl - 1) + (plan.x - 1) * plan.zl
    per_rol = (plan.zh - 1) + (plan.y - 1) * plan.zh + plan.zh * plan.y

    def send(buf, index, piece, device, ssem, rsem, number):
        ref = slot(buf, index, piece)
        pltpu.make_async_remote_copy(
            src_ref=ref,
            dst_ref=ref,
            send_sem=ssem.at[number],
            recv_sem=rsem.at[index, piece],
            device_id=device,
            device_id_type=MESH,
        ).start()

    def arrived(buf, index, piece, ssem, rsem):
        ref = slot(buf, index, piece)
        pltpu.make_async_remote_copy(
            src_ref=ref,
            dst_ref=ref,
            send_sem=ssem.at[0],
            recv_sem=rsem.at[index, piece],
            device_id=partner,
            device_id_type=MESH,
        ).wait_recv()

    def each_piece(run):
        def step(k, carry):
            counts = [k * per_dem, k * per_rol]

            def dem_on(index, device):
                send(dem, index, k, device, s_dem, r_dem, counts[0])
                counts[0] += 1

            def rol_on(index, device):
                send(rol, index, k, device, s_rol, r_rol, counts[1])
                counts[1] += 1

            run(k, counts, dem_on, rol_on)
            return carry

        lax.fori_loop(0, plan.pieces, step, 0)

    def first_hop(k, counts, dem_on, rol_on):
        for dz in range(1, plan.zl):
            dem_on(p_me, row_peers[(dz, 0)][0])
        for dz in range(1, plan.zh):
            rol_on(q_me, col_peers[(dz, 0, 0)][0])
        for dx in range(1, plan.x):
            dem_on(p_me, row_peers[(0, dx)][0])
        for dy in range(1, plan.y):
            rol_on(q_me, col_peers[(0, dy, 0)][0])
        rol_on(q_me, partner)

    first_dem = (plan.zl - 1) + (plan.x - 1)
    first_rol = (plan.zh - 1) + (plan.y - 1) + 1

    def second_hop(k, counts, dem_on, rol_on):
        counts[0] += first_dem
        counts[1] += first_rol
        for dz in range(1, plan.zl):
            index = row_peers[(dz, 0)][1]
            arrived(dem, index, k, s_dem, r_dem)
            for dx in range(1, plan.x):
                dem_on(index, row_peers[(0, dx)][0])
        for dz in range(1, plan.zh):
            index = col_peers[(dz, 0, 0)][1]
            arrived(rol, index, k, s_rol, r_rol)
            for dy in range(1, plan.y):
                rol_on(index, col_peers[(0, dy, 0)][0])
            rol_on(index, partner)
        for dy in range(1, plan.y):
            index = col_peers[(0, dy, 0)][1]
            arrived(rol, index, k, s_rol, r_rol)
            rol_on(index, partner)

    second_rol = (plan.zh - 1) * plan.y + (plan.y - 1)

    def relay(k, counts, dem_on, rol_on):
        counts[1] += first_rol + second_rol
        for dz in range(1, plan.zh):
            for dy in range(1, plan.y):
                index = col_peers[(dz, dy, 0)][1]
                arrived(rol, index, k, s_rol, r_rol)
                rol_on(index, partner)
        for dz in range(plan.zl):
            for dx in range(1, plan.x):
                arrived(dem, row_peers[(dz, dx)][1], k, s_dem, r_dem)

    each_piece(first_hop)
    each_piece(second_hop)
    each_piece(relay)

    def lanes(c):
        return slice(c * LANES, (c + 1) * LANES)

    def group(r):
        return pl.ds(pl.multiple_of(r * SUB, SUB), SUB)

    def over(h, body, init, unroll):
        first = h * (chunk // BLOCK)
        return lax.fori_loop(first, first + chunk // BLOCK, body, init, unroll=unroll)

    eye = lax.broadcasted_iota(jnp.int32, (LANES, LANES), 0) == lax.broadcasted_iota(
        jnp.int32, (LANES, LANES), 1
    )

    def to_lanes(column):
        return jnp.sum(jnp.where(eye, column, 0.0), axis=0, keepdims=True)

    pair = 2 * blk // LANES

    def at(here, c):
        return dist[c // pair, here, lanes(c % pair)]

    def columns(place, carry):
        zz, yy = lax.rem(zhi + place // plan.y, plan.zh), lax.rem(y + place % plan.y, plan.y)
        index = (zz * plan.y + yy) * 2

        def piece_in(k, c):
            arrived(rol, index + (1 - core), k, s_rol, r_rol)
            return c

        lax.fori_loop(0, plan.pieces, piece_in, 0)

        def unit(where, carry):
            first = pl.multiple_of(where * blk, 16)
            for c in range(2):
                other = index + (core if c == 0 else 1 - core)
                inner = lax.dot_general(
                    dem[pl.ds(first, blk), :],
                    rol[pl.ds(pl.multiple_of(other * blk, 16), blk), :],
                    (((1,), (1,)), ((), ())),
                    preferred_element_type=jnp.float32,
                )
                dist[place, pl.ds(first, blk), c * blk : (c + 1) * blk] = (1.0 - inner) * (
                    1.0 / EPS
                )

            def step(r, carry):
                here = pl.ds(pl.multiple_of(first + r * SUB, SUB), SUB)
                values = [dist[place, here, lanes(c)] for c in range(pair)]
                before = best[here, :]
                low = jnp.minimum(before, tree(jnp.minimum, values))
                total = tree(jnp.add, [jnp.exp(low - v) for v in values])
                part[here, :] = total + part[here, :] * jnp.exp(low - before)
                best[here, :] = low
                return carry

            return lax.fori_loop(0, blk // SUB, step, carry, unroll=min(16, blk // SUB))

        return lax.fori_loop(0, plan.gr, unit, carry)

    def store_line(buf, index, first, k, line):
        at = k * LANES
        done = 0
        while done < LANES:
            i, j = (at + done) // blk, (at + done) % blk
            n = min(LANES - done, blk - j)
            buf[index, first, i : i + 1, j : j + n] = line[:, done : done + n]
            done += n

    def shared(buf, index, device, ssem, rsem, i, h):
        ref = buf.at[index, h]
        return pltpu.make_async_remote_copy(
            src_ref=ref,
            dst_ref=ref,
            send_sem=ssem.at[i, h],
            recv_sem=rsem.at[index, h],
            device_id=device,
            device_id_type=MESH,
        )

    def exchange_start(buf, index, others, ssem, rsem, h):
        for i, (device, _) in enumerate(others):
            shared(buf, index, device, ssem, rsem, i, h).start()

    def exchange_wait(buf, others, ssem, rsem, h):
        for i, (device, other) in enumerate(others):
            shared(buf, other, device, ssem, rsem, i, h).wait_recv()

    def exchange_sent(buf, index, others, ssem, rsem, h):
        for i, (device, _) in enumerate(others):
            shared(buf, index, device, ssem, rsem, i, h).wait_send()

    def log_total(values):
        top = tree(jnp.maximum, values)
        return top + jnp.log(tree(jnp.add, [jnp.exp(v - top) for v in values]))

    def line_of(pieces):
        return pieces[0] if len(pieces) == 1 else jnp.concatenate(pieces, axis=1)

    def spread(h, values):
        line = line_of([values[i : i + 1, :] for i in range(values.shape[0])])
        for k in range(chunk // LANES):
            column = jnp.sum(jnp.where(eye, line[:, lanes(k)], 0.0), axis=1, keepdims=True)
            start = pl.multiple_of(h * chunk + k * LANES, LANES)
            wide[pl.ds(start, LANES), :] = jnp.broadcast_to(column, (LANES, LANES))

    per_chunk = chunk // LANES
    slots = chunk // blk
    log_n = math.log(plan.total)

    def each_chunk(run):
        def step(h, carry):
            run(h)
            return carry

        lax.fori_loop(0, chunks, step, 0)

    best[...] = jnp.full_like(best, 1e30)
    part[...] = jnp.zeros_like(part)
    lax.fori_loop(0, plan.zh * plan.y, columns, 0)

    def first_f(h):
        for k in range(per_chunk):
            here = pl.ds(pl.multiple_of(h * chunk + k * LANES, LANES), LANES)
            low = best[here, :]
            least = jnp.min(low, axis=1, keepdims=True)
            total = jnp.sum(part[here, :] * jnp.exp(least - low), axis=1, keepdims=True)
            store_line(lf1, p_me, h, k, jnp.log(to_lanes(total)) - to_lanes(least))
        exchange_start(lf1, p_me, row_others, s_f1, r_f1, h)

    each_chunk(first_f)

    def inside(b, g):
        return pl.ds(pl.multiple_of(b * BLOCK + g * SUB, SUB), SUB)

    def col_sum(b, carry):
        f_here = [wide[inside(b, g), :] for g in range(GROUPS)]
        for c in range(n_parts):
            values = [f_here[g] - at(inside(b, g), c) for g in range(GROUPS)]
            top = tree(jnp.maximum, values)
            values = [jnp.exp(v - top) for v in values]
            for g in range(GROUPS):
                kern[inside(b, g), lanes(c)] = values[g]
            tops[group(b), lanes(c)] = top
            sums[group(b), lanes(c)] = tree(jnp.add, values)
        return carry

    def first_g(h):
        exchange_wait(lf1, row_others, s_f1, r_f1, h)
        f_all[h] = -log_n - log_total([lf1[i, h] for i in range(plan.gr)])
        spread(h, f_all[h])
        over(h, col_sum, 0, 1)

    each_chunk(first_g)
    blocks = rows // BLOCK
    low_all = tuple(jnp.full((SUB, LANES), -1e30, jnp.float32) for _ in range(n_parts))
    top_all = lax.fori_loop(
        0,
        blocks,
        lambda b, m: tuple(jnp.maximum(m[c], tops[group(b), lanes(c)]) for c in range(n_parts)),
        low_all,
        unroll=4,
    )
    sum_all = lax.fori_loop(
        0,
        blocks,
        lambda b, t: tuple(
            t[c] + sums[group(b), lanes(c)] * jnp.exp(tops[group(b), lanes(c)] - top_all[c])
            for c in range(n_parts)
        ),
        tuple(jnp.zeros((SUB, LANES), jnp.float32) for _ in range(n_parts)),
        unroll=4,
    )
    pieces = []
    for c in range(n_parts):
        top = jnp.max(top_all[c], axis=0, keepdims=True)
        total = jnp.sum(sum_all[c] * jnp.exp(top_all[c] - top), axis=0, keepdims=True)
        pieces.append(top + jnp.log(total))
    line = line_of(pieces)
    for i, place in enumerate(places):
        lg[q_me, 0, pl.ds(place, 1), :] = line[:, i * blk : (i + 1) * blk]
    exchange_start(lg, q_me, col_others, s_g, r_g, 0)
    exchange_wait(lg, col_others, s_g, r_g, 0)
    g_all[...] = -log_n - log_total([lg[i, 0] for i in range(plan.gc)])
    g_line = line_of([g_all[pl.ds(place, 1), :] for place in places])

    def rescale(b, carry):
        tops[group(b), :] = jnp.exp(tops[group(b), :] + g_line)
        return carry

    lax.fori_loop(0, blocks, rescale, 0, unroll=4)

    def second_rows(b, carry):
        totals = [None] * GROUPS
        for c in range(n_parts):
            scale = tops[group(b), lanes(c)]
            for g in range(GROUPS):
                value = kern[inside(b, g), lanes(c)] * scale
                totals[g] = value if c == 0 else totals[g] + value
        for g in range(GROUPS):
            part[inside(b, g), :] = totals[g]
        return carry

    def second_f(h):
        over(h, second_rows, 0, 1)
        for k in range(per_chunk):
            here = pl.ds(pl.multiple_of(h * chunk + k * LANES, LANES), LANES)
            total = jnp.sum(part[here, :], axis=1, keepdims=True)
            store_line(lf2, p_me, h, k, to_lanes(total))
        exchange_start(lf2, p_me, row_others, s_f2, r_f2, h)

    each_chunk(second_f)

    def last(b, carry):
        u_here = [wide[inside(b, g), :] for g in range(GROUPS)]
        for c in range(n_parts):
            scale = tops[group(b), lanes(c)]
            values = [u_here[g] * kern[inside(b, g), lanes(c)] for g in range(GROUPS)]
            mass_c[:, lanes(c)] += tree(jnp.add, values) * scale
            values = [values[g] * at(inside(b, g), c) for g in range(GROUPS)]
            cost_c[:, lanes(c)] += tree(jnp.add, values) * scale
        return carry

    mass_c[...] = jnp.zeros_like(mass_c)
    cost_c[...] = jnp.zeros_like(cost_c)

    def second_g(h):
        exchange_wait(lf2, row_others, s_f2, r_f2, h)
        mass = tree(jnp.add, [lf2[i, h] for i in range(plan.gr)]) * float(plan.total)
        spread(h, 1.0 / mass)
        f_all[h] = f_all[h] - jnp.log(mass)
        over(h, last, 0, 1)

    each_chunk(second_g)
    both = jnp.concatenate(
        [
            jnp.sum(mass_c[...], axis=0, keepdims=True),
            jnp.sum(cost_c[...], axis=0, keepdims=True),
        ],
        axis=0,
    )
    for i, place in enumerate(places):
        cw_out[place] = both[:, i * blk : (i + 1) * blk]
    for i, (device, other) in enumerate(col_others):
        copy = pltpu.make_async_remote_copy(
            src_ref=cw_out.at[other],
            dst_ref=cw_in.at[q_me],
            send_sem=s_c.at[i],
            recv_sem=r_c.at[q_me],
            device_id=device,
            device_id_type=MESH,
        )
        copy.start()
        started.append(copy)
    cw_in[q_me] = cw_out[q_me]
    for i, (device, other) in enumerate(col_others):
        pltpu.make_async_remote_copy(
            src_ref=cw_out.at[other],
            dst_ref=cw_in.at[other],
            send_sem=s_c.at[i],
            recv_sem=r_c.at[other],
            device_id=device,
            device_id_type=MESH,
        ).wait_recv()
    total = tree(jnp.add, [cw_in[i] for i in range(plan.gc)])
    out_ref[0:1, :] = f_all[p_me // slots, pl.ds(lax.rem(p_me, slots), 1), :]
    out_ref[1:2, :] = g_all[pl.ds(q_me, 1), :] - jnp.log(total[0:1] * float(plan.total))
    out_ref[2:3, :] = total[1:2] / total[0:1] * -EPS
    for copy in started:
        copy.wait_send()
    for h in range(chunks):
        exchange_sent(lf1, p_me, row_others, s_f1, r_f1, h)
        exchange_sent(lf2, p_me, row_others, s_f2, r_f2, h)
    exchange_sent(lg, q_me, col_others, s_g, r_g, 0)

    def sent(buf, index, ssem, rsem, count):
        ref = slot(buf, index, 0)

        def step(i, carry):
            pltpu.make_async_remote_copy(
                src_ref=ref,
                dst_ref=ref,
                send_sem=ssem.at[i],
                recv_sem=rsem.at[index, 0],
                device_id=partner,
                device_id_type=MESH,
            ).wait_send()
            return carry

        lax.fori_loop(0, count, step, 0)

    sent(dem, p_me, s_dem, r_dem, plan.pieces * per_dem)
    sent(rol, q_me, s_rol, r_rol, plan.pieces * per_rol)


def body(plan, demo, rollout):
    blk, width, rows, cols = plan.blk, plan.width, plan.rows, plan.cols
    n_dem = plan.pieces * ((plan.zl - 1) + (plan.x - 1) * plan.zl)
    n_rol = plan.pieces * (
        (plan.zh - 1) + (plan.y - 1) * plan.zh + plan.zh * plan.y
    )
    dma = pltpu.SemaphoreType.DMA
    f32 = jnp.float32
    out = pl.pallas_call(
        functools.partial(kernel, plan),
        out_shape=jax.ShapeDtypeStruct((3, blk), f32),
        in_specs=[pl.BlockSpec(memory_space=pltpu.HBM)] * 2,
        out_specs=pl.BlockSpec(memory_space=pltpu.VMEM),
        scratch_shapes=[
            pltpu.VMEM((blk, width), jnp.bfloat16),
            pltpu.VMEM((blk, width), jnp.bfloat16),
            pltpu.VMEM((rows, width), jnp.bfloat16),
            pltpu.VMEM((cols, width), jnp.bfloat16),
            pltpu.VMEM((plan.zh * plan.y, rows, 2 * blk), f32),
            pltpu.VMEM((rows, cols), f32),
            pltpu.VMEM((rows, LANES), f32),
            pltpu.VMEM((rows, LANES), f32),
            pltpu.VMEM((rows, LANES), f32),
            pltpu.VMEM((rows // GROUPS, cols), f32),
            pltpu.VMEM((rows // GROUPS, cols), f32),
            pltpu.VMEM((SUB, cols), f32),
            pltpu.VMEM((SUB, cols), f32),
            pltpu.VMEM((plan.gr, plan.chunks, plan.gr // plan.chunks, blk), f32),
            pltpu.VMEM((plan.gr, plan.chunks, plan.gr // plan.chunks, blk), f32),
            pltpu.VMEM((plan.gc, 1, plan.gc, blk), f32),
            pltpu.VMEM((plan.chunks, plan.gr // plan.chunks, blk), f32),
            pltpu.VMEM((plan.gc, blk), f32),
            pltpu.VMEM((plan.gc, 2, blk), f32),
            pltpu.VMEM((plan.gc, 2, blk), f32),
            dma((2,)),
            dma((n_dem,)),
            dma((plan.gr, plan.pieces)),
            dma((n_rol,)),
            dma((plan.gc, plan.pieces)),
            dma((plan.gr, plan.chunks)),
            dma((plan.gr, plan.chunks)),
            dma((plan.gr, plan.chunks)),
            dma((plan.gr, plan.chunks)),
            dma((plan.gc, 1)),
            dma((plan.gc, 1)),
            dma((plan.gc,)),
            dma((plan.gc,)),
        ],
        compiler_params=pltpu.CompilerParams(
            collective_id=0, has_side_effects=True, vmem_limit_bytes=64 * 1024 * 1024 - 128 * 1024
        ),
    )(demo, rollout)
    return out[0], out[1], out[2]


def solution(mesh):
    rows_axis, cols_axis = mesh.shape["row"], mesh.shape["col"]

    def run(demo, rollout):
        blk = demo.shape[0] // (rows_axis * cols_axis)
        plan = Plan(rows_axis, cols_axis, blk, demo.shape[1])
        return jax.shard_map(
            functools.partial(body, plan),
            mesh=mesh,
            in_specs=(P(("row", "col"), None), P(("row", "col"), None)),
            out_specs=(P(("row", "col")), P(("row", "col")), P(("row", "col"))),
            check_vma=False,
        )(demo, rollout)

    return run
```

```python
import functools
import math

import jax
import jax.numpy as jnp
from jax import lax
from jax.experimental import pallas as pl
from jax.experimental.pallas import tpu as pltpu
from jax.sharding import PartitionSpec as P

EPS = 0.005
MESH = pl.DeviceIdType.MESH
LANES = 128
SUB = 8
GROUPS = 8
BLOCK = SUB * GROUPS


class Plan:
    def __init__(self, rows_axis, cols_axis, blk, width):
        self.core = 2
        depth = rows_axis // 2
        self.x = 1 << ((cols_axis.bit_length() - 1) // 2)
        self.y = cols_axis // self.x
        self.zl = min(depth, max(1, cols_axis // self.x))
        self.zh = depth // self.zl
        self.blk = blk
        self.width = width
        self.gr = self.zl * self.x
        self.gc = self.zh * self.y * self.core
        self.rows = self.gr * blk
        self.cols = self.gc * blk
        self.total = rows_axis * cols_axis * blk
        self.pieces = max(1, min(4, blk // 16))
        self.piece = blk // self.pieces
        self.fine = blk % LANES == 0 and (self.zl, self.x, self.zh, self.y, self.pieces) == (2, 2, 2, 2, 4)
        self.chunks = 2 if blk % LANES == 0 and self.gr % 2 == 0 else 1


def normalize(embed):
    values = embed.astype(jnp.float32)
    inverse = lax.rsqrt(jnp.sum(values * values, axis=-1, keepdims=True) + 1e-06)
    return (values * inverse).astype(jnp.bfloat16)


def tree(op, items):
    items = list(items)
    while len(items) > 1:
        items = [
            op(items[i], items[i + 1]) if i + 1 < len(items) else items[i]
            for i in range(0, len(items), 2)
        ]
    return items[0]


def kernel(
    plan,
    demo_hbm,
    roll_hbm,
    out_ref,
    demo_ref,
    roll_ref,
    dem,
    rol,
    dist,
    kern,
    best,
    part,
    wide,
    tops,
    sums,
    mass_c,
    cost_c,
    lf1,
    lf2,
    lg,
    f_all,
    g_all,
    cw_out,
    cw_in,
    s_in,
    s_dem,
    r_dem,
    s_rol,
    r_rol,
    s_f1,
    r_f1,
    s_f2,
    r_f2,
    s_g,
    r_g,
    s_c,
    r_c,
):
    blk, rows, cols = plan.blk, plan.rows, plan.cols
    n_parts = cols // LANES
    chunks, chunk = plan.chunks, rows // plan.chunks
    row = lax.axis_index("row")
    col = lax.axis_index("col")
    core, z = lax.rem(row, 2), row // 2
    zlo, zhi = lax.rem(z, plan.zl), z // plan.zl
    x, y = lax.rem(col, plan.x), col // plan.x

    load_demo = pltpu.make_async_copy(demo_hbm, demo_ref, s_in.at[0])
    load_roll = pltpu.make_async_copy(roll_hbm, roll_ref, s_in.at[1])
    load_demo.start()
    load_roll.start()

    def row_peer(dz, dx):
        zz, xx = lax.rem(zlo + dz, plan.zl), lax.rem(x + dx, plan.x)
        device = ((zhi * plan.zl + zz) * 2 + core, y * plan.x + xx)
        return device, zz * plan.x + xx

    def col_peer(dz, dy, dc):
        zz, yy, cc = lax.rem(zhi + dz, plan.zh), lax.rem(y + dy, plan.y), lax.rem(core + dc, 2)
        device = ((zz * plan.zl + zlo) * 2 + cc, yy * plan.x + x)
        return device, (zz * plan.y + yy) * 2 + cc

    row_offsets = [(a, b) for a in range(plan.zl) for b in range(plan.x)]
    col_offsets = [(a, b, c) for a in range(plan.zh) for b in range(plan.y) for c in range(2)]
    row_peers = {o: row_peer(*o) for o in row_offsets}
    col_peers = {o: col_peer(*o) for o in col_offsets}
    p_me = row_peers[(0, 0)][1]
    q_me = col_peers[(0, 0, 0)][1]
    row_others = [row_peers[o] for o in row_offsets[1:]]
    col_others = [col_peers[o] for o in col_offsets[1:]]
    places = [col_peers[o][1] for o in col_offsets]

    barrier = pltpu.get_barrier_semaphore()
    for device, _ in row_others + col_others:
        pl.semaphore_signal(barrier, inc=1, device_id=device, device_id_type=MESH)

    def slot(buf, index, piece):
        start = pl.multiple_of(index * blk + piece * plan.piece, 16)
        return buf.at[pl.ds(start, plan.piece), :]

    load_demo.wait()
    dem[pl.ds(pl.multiple_of(p_me * blk, 16), blk), :] = normalize(demo_ref[...])
    load_roll.wait()
    rol[pl.ds(pl.multiple_of(q_me * blk, 16), blk), :] = normalize(roll_ref[...])
    pl.semaphore_wait(barrier, len(row_others) + len(col_others))

    partner = col_peers[(0, 0, 1)][0]
    started = []

    def send(buf, index, piece, device, ssem, rsem, count):
        ref = slot(buf, index, piece)
        copy = pltpu.make_async_remote_copy(
            src_ref=ref,
            dst_ref=ref,
            send_sem=ssem.at[count[0]],
            recv_sem=rsem.at[index, piece],
            device_id=device,
            device_id_type=MESH,
        )
        copy.start()
        count[0] += 1
        started.append(copy)

    def arrived(buf, index, piece, ssem, rsem):
        ref = slot(buf, index, piece)
        pltpu.make_async_remote_copy(
            src_ref=ref,
            dst_ref=ref,
            send_sem=ssem.at[0],
            recv_sem=rsem.at[index, piece],
            device_id=partner,
            device_id_type=MESH,
        ).wait_recv()

    n_dem, n_rol = [0], [0]
    send_dem = lambda i, k, d: send(dem, i, k, d, s_dem, r_dem, n_dem)
    send_rol = lambda i, k, d: send(rol, i, k, d, s_rol, r_rol, n_rol)
    for k in range(plan.pieces):
        for dz in range(1, plan.zl):
            send_dem(p_me, k, row_peers[(dz, 0)][0])
        for dz in range(1, plan.zh):
            send_rol(q_me, k, col_peers[(dz, 0, 0)][0])
        for dx in range(1, plan.x):
            send_dem(p_me, k, row_peers[(0, dx)][0])
        for dy in range(1, plan.y):
            send_rol(q_me, k, col_peers[(0, dy, 0)][0])
        send_rol(q_me, k, partner)
    def lanes(c):
        return slice(c * LANES, (c + 1) * LANES)

    def group(r):
        return pl.ds(pl.multiple_of(r * SUB, SUB), SUB)

    def over(h, body, init, unroll):
        first = h * chunk // BLOCK
        return lax.fori_loop(first, first + chunk // BLOCK, body, init, unroll=unroll)

    def total_line(k, size):
        return lax.dot_general(
            jnp.ones((SUB, LANES), jnp.float32),
            part[k * LANES : k * LANES + size, :],
            (((1,), (1,)), ((), ())),
            precision=lax.Precision.HIGHEST,
            preferred_element_type=jnp.float32,
        )[0:1, :]

    def tile(where, place):
        first = 0 if where is None else pl.multiple_of(where * blk, 16)
        here = pl.ds(first, rows if where is None else blk)
        for i in range(2 * place, 2 * place + 2):
            inner = lax.dot_general(
                dem[here, :],
                rol[pl.ds(pl.multiple_of(places[i] * blk, 16), blk), :],
                (((1,), (1,)), ((), ())),
                preferred_element_type=jnp.float32,
            )
            dist[here, i * blk : (i + 1) * blk] = (1.0 - inner) * (1.0 / EPS)

    def row_stats(first_row, size, place):
        pair = 2 * blk // LANES

        def step(r, carry):
            here = pl.ds(pl.multiple_of(first_row + r * SUB, SUB), SUB)
            values = [dist[here, lanes(c)] for c in range(place * pair, (place + 1) * pair)]
            low = tree(jnp.minimum, values)
            if place > 0:
                before = best[here, :]
                low = jnp.minimum(low, before)
            total = tree(jnp.add, [jnp.exp(low - v) for v in values])
            if place > 0:
                total = total + part[here, :] * jnp.exp(low - before)
            best[here, :] = low
            part[here, :] = total
            return carry

        lax.fori_loop(0, size // SUB, step, 0, unroll=16)

    def unit(where, place):
        tile(where, place)
        row_stats(pl.multiple_of(where * blk, SUB), blk, place)

    def store_line(buf, index, k, line):
        at = k * LANES
        done = 0
        while done < LANES:
            i, j = (at + done) // blk, (at + done) % blk
            n = min(LANES - done, blk - j)
            buf[index, i : i + 1, j : j + n] = line[:, done : done + n]
            done += n

    def exchange_start(buf, index, others, ssem, rsem, h, slots):
        here = pl.ds(h * slots, slots)
        for i, (device, _) in enumerate(others):
            copy = pltpu.make_async_remote_copy(
                src_ref=buf.at[index, here],
                dst_ref=buf.at[index, here],
                send_sem=ssem.at[i, h],
                recv_sem=rsem.at[index, h],
                device_id=device,
                device_id_type=MESH,
            )
            copy.start()
            started.append(copy)

    def exchange_wait(buf, others, ssem, rsem, h, slots):
        here = pl.ds(h * slots, slots)
        for i, (device, other) in enumerate(others):
            pltpu.make_async_remote_copy(
                src_ref=buf.at[other, here],
                dst_ref=buf.at[other, here],
                send_sem=ssem.at[i, h],
                recv_sem=rsem.at[other, h],
                device_id=device,
                device_id_type=MESH,
            ).wait_recv()

    def log_total(values):
        top = tree(jnp.maximum, values)
        return top + jnp.log(tree(jnp.add, [jnp.exp(v - top) for v in values]))

    def line_of(pieces):
        return pieces[0] if len(pieces) == 1 else jnp.concatenate(pieces, axis=1)

    def spread(h, values):
        line = line_of([values[i : i + 1, :] for i in range(values.shape[0])])
        first = lax.broadcasted_iota(jnp.int32, (SUB, chunk), 0) == 0
        wide[h * chunk : (h + 1) * chunk, :] = lax.dot_general(
            jnp.where(first, line, 0.0),
            jnp.ones((SUB, LANES), jnp.float32),
            (((0,), (0,)), ((), ())),
            precision=lax.Precision.HIGHEST,
            preferred_element_type=jnp.float32,
        )

    per_chunk = chunk // LANES
    slots = chunk // blk
    log_n = math.log(plan.total)

    def forward(k):
        for dz in range(1, plan.zl):
            index = row_peers[(dz, 0)][1]
            arrived(dem, index, k, s_dem, r_dem)
            for dx in range(1, plan.x):
                send_dem(index, k, row_peers[(0, dx)][0])
        for dz in range(1, plan.zh):
            index = col_peers[(dz, 0, 0)][1]
            arrived(rol, index, k, s_rol, r_rol)
            for dy in range(1, plan.y):
                send_rol(index, k, col_peers[(0, dy, 0)][0])
            send_rol(index, k, partner)
        for dy in range(1, plan.y):
            index = col_peers[(0, dy, 0)][1]
            arrived(rol, index, k, s_rol, r_rol)
            send_rol(index, k, partner)

    def relay():
        for k in range(plan.pieces):
            for dz in range(1, plan.zh):
                for dy in range(1, plan.y):
                    index = col_peers[(dz, dy, 0)][1]
                    arrived(rol, index, k, s_rol, r_rol)
                    send_rol(index, k, partner)

    def rows_in(dz, dx):
        index = row_peers[(dz, dx)][1]
        for k in range(plan.pieces):
            arrived(dem, index, k, s_dem, r_dem)
        return index

    def cols_in(dz, dy):
        for k in range(plan.pieces):
            arrived(rol, col_peers[(dz, dy, 1)][1], k, s_rol, r_rol)

    if plan.fine:
        own, near_y, near_z, far = range(4)
        cols_in(0, 0)
        unit(p_me, own)
        forward(0)
        forward(1)
        row_x = rows_in(0, 1)
        unit(row_x, own)
        forward(2)
        forward(3)
        row_z = row_peers[(1, 0)][1]
        cols_in(0, 1)
        unit(p_me, near_y)
        unit(row_z, own)
        relay()
        unit(row_x, near_y)
        unit(row_z, near_y)
        cols_in(1, 0)
        for index in (p_me, row_x, row_z):
            unit(index, near_z)
        row_f = rows_in(1, 1)
        for place in (own, near_y, near_z):
            unit(row_f, place)
        cols_in(1, 1)
        tile(None, far)
        last_place = far
    else:
        for k in range(plan.pieces):
            forward(k)
        relay()
        for dz in range(plan.zl):
            for dx in range(1, plan.x):
                rows_in(dz, dx)
        last_place = len(places) // 2 - 1
        for place in range(last_place + 1):
            cols_in(*col_offsets[2 * place][:2])
            tile(None, place)
            if place < last_place:
                row_stats(0, rows, place)

    for h in range(chunks):
        row_stats(h * chunk, chunk, last_place)
        for k in range(h * per_chunk, (h + 1) * per_chunk):
            low = best[lanes(k), :].T
            least = jnp.min(low, axis=0, keepdims=True)
            total = jnp.sum(part[lanes(k), :].T * jnp.exp(least - low), axis=0, keepdims=True)
            store_line(lf1, p_me, k, jnp.log(total) - least)
        exchange_start(lf1, p_me, row_others, s_f1, r_f1, h, slots)

    def inside(b, g):
        return pl.ds(pl.multiple_of(b * BLOCK + g * SUB, SUB), SUB)

    def col_sum(b, carry):
        f_here = [wide[inside(b, g), :] for g in range(GROUPS)]
        for c in range(n_parts):
            values = [f_here[g] - dist[inside(b, g), lanes(c)] for g in range(GROUPS)]
            top = tree(jnp.maximum, values)
            values = [jnp.exp(v - top) for v in values]
            for g in range(GROUPS):
                kern[inside(b, g), lanes(c)] = values[g]
            tops[group(b), lanes(c)] = top
            sums[group(b), lanes(c)] = tree(jnp.add, values)
        return carry

    for h in range(chunks):
        exchange_wait(lf1, row_others, s_f1, r_f1, h, slots)
        here = pl.ds(h * slots, slots)
        f_all[here, :] = -log_n - log_total([lf1[i, here, :] for i in range(plan.gr)])
        spread(h, f_all[here, :])
        over(h, col_sum, 0, 1)

    blocks = rows // BLOCK
    pieces = []
    for c in range(n_parts):
        top = tree(jnp.maximum, [tops[b * SUB : (b + 1) * SUB, lanes(c)] for b in range(blocks)])
        top = jnp.max(top, axis=0, keepdims=True)
        total = tree(
            jnp.add,
            [
                sums[b * SUB : (b + 1) * SUB, lanes(c)]
                * jnp.exp(tops[b * SUB : (b + 1) * SUB, lanes(c)] - top)
                for b in range(blocks)
            ],
        )
        pieces.append(top + jnp.log(jnp.sum(total, axis=0, keepdims=True)))
    line = line_of(pieces)
    for i, place in enumerate(places):
        lg[q_me, pl.ds(place, 1), :] = line[:, i * blk : (i + 1) * blk]
    exchange_start(lg, q_me, col_others, s_g, r_g, 0, plan.gc)
    exchange_wait(lg, col_others, s_g, r_g, 0, plan.gc)
    g_all[...] = -log_n - log_total([lg[i] for i in range(plan.gc)])
    g_line = line_of([g_all[pl.ds(place, 1), :] for place in places])
    for c in range(n_parts):
        tops[:, lanes(c)] = jnp.exp(tops[:, lanes(c)] + g_line[:, lanes(c)])

    def second_rows(b, carry):
        totals = [None] * GROUPS
        for c in range(n_parts):
            scale = tops[group(b), lanes(c)]
            for g in range(GROUPS):
                value = kern[inside(b, g), lanes(c)] * scale
                totals[g] = value if c == 0 else totals[g] + value
        for g in range(GROUPS):
            part[inside(b, g), :] = totals[g]
        return carry

    for h in range(chunks):
        over(h, second_rows, 0, 1)
        line = total_line(h * per_chunk, chunk)
        for k in range(per_chunk):
            store_line(lf2, p_me, h * per_chunk + k, line[:, lanes(k)])
        exchange_start(lf2, p_me, row_others, s_f2, r_f2, h, slots)

    def last(b, carry):
        u_here = [wide[inside(b, g), :] for g in range(GROUPS)]
        for c in range(n_parts):
            scale = tops[group(b), lanes(c)]
            values = [u_here[g] * kern[inside(b, g), lanes(c)] for g in range(GROUPS)]
            mass_c[:, lanes(c)] += tree(jnp.add, values) * scale
            values = [values[g] * dist[inside(b, g), lanes(c)] for g in range(GROUPS)]
            cost_c[:, lanes(c)] += tree(jnp.add, values) * scale
        return carry

    mass_c[...] = jnp.zeros_like(mass_c)
    cost_c[...] = jnp.zeros_like(cost_c)
    for h in range(chunks):
        exchange_wait(lf2, row_others, s_f2, r_f2, h, slots)
        here = pl.ds(h * slots, slots)
        mass = tree(jnp.add, [lf2[i, here, :] for i in range(plan.gr)]) * float(plan.total)
        spread(h, 1.0 / mass)
        f_all[here, :] = f_all[here, :] - jnp.log(mass)
        over(h, last, 0, 1)

    both = jnp.concatenate(
        [
            jnp.sum(mass_c[...], axis=0, keepdims=True),
            jnp.sum(cost_c[...], axis=0, keepdims=True),
        ],
        axis=0,
    )
    for i, place in enumerate(places):
        cw_out[place] = both[:, i * blk : (i + 1) * blk]
    for i, (device, other) in enumerate(col_others):
        copy = pltpu.make_async_remote_copy(
            src_ref=cw_out.at[other],
            dst_ref=cw_in.at[q_me],
            send_sem=s_c.at[i],
            recv_sem=r_c.at[q_me],
            device_id=device,
            device_id_type=MESH,
        )
        copy.start()
        started.append(copy)
    cw_in[q_me] = cw_out[q_me]
    for i, (device, other) in enumerate(col_others):
        pltpu.make_async_remote_copy(
            src_ref=cw_out.at[other],
            dst_ref=cw_in.at[other],
            send_sem=s_c.at[i],
            recv_sem=r_c.at[other],
            device_id=device,
            device_id_type=MESH,
        ).wait_recv()
    total = tree(jnp.add, [cw_in[i] for i in range(plan.gc)])
    out_ref[0:1, :] = f_all[pl.ds(p_me, 1), :]
    out_ref[1:2, :] = g_all[pl.ds(q_me, 1), :] - jnp.log(total[0:1] * float(plan.total))
    out_ref[2:3, :] = total[1:2] / total[0:1] * -EPS
    for copy in started:
        copy.wait_send()


def body(plan, demo, rollout):
    blk, width, rows, cols = plan.blk, plan.width, plan.rows, plan.cols
    n_dem = plan.pieces * ((plan.zl - 1) + (plan.x - 1) * plan.zl)
    n_rol = plan.pieces * (
        (plan.zh - 1) + (plan.y - 1) * plan.zh + plan.zh * plan.y
    )
    dma = pltpu.SemaphoreType.DMA
    f32 = jnp.float32
    out = pl.pallas_call(
        functools.partial(kernel, plan),
        out_shape=jax.ShapeDtypeStruct((3, blk), f32),
        in_specs=[pl.BlockSpec(memory_space=pltpu.HBM)] * 2,
        out_specs=pl.BlockSpec(memory_space=pltpu.VMEM),
        scratch_shapes=[
            pltpu.VMEM((blk, width), jnp.bfloat16),
            pltpu.VMEM((blk, width), jnp.bfloat16),
            pltpu.VMEM((rows, width), jnp.bfloat16),
            pltpu.VMEM((cols, width), jnp.bfloat16),
            pltpu.VMEM((rows, cols), f32),
            pltpu.VMEM((rows, cols), f32),
            pltpu.VMEM((rows, LANES), f32),
            pltpu.VMEM((rows, LANES), f32),
            pltpu.VMEM((rows, LANES), f32),
            pltpu.VMEM((rows // GROUPS, cols), f32),
            pltpu.VMEM((rows // GROUPS, cols), f32),
            pltpu.VMEM((SUB, cols), f32),
            pltpu.VMEM((SUB, cols), f32),
            pltpu.VMEM((plan.gr, plan.gr, blk), f32),
            pltpu.VMEM((plan.gr, plan.gr, blk), f32),
            pltpu.VMEM((plan.gc, plan.gc, blk), f32),
            pltpu.VMEM((plan.gr, blk), f32),
            pltpu.VMEM((plan.gc, blk), f32),
            pltpu.VMEM((plan.gc, 2, blk), f32),
            pltpu.VMEM((plan.gc, 2, blk), f32),
            dma((2,)),
            dma((n_dem,)),
            dma((plan.gr, plan.pieces)),
            dma((n_rol,)),
            dma((plan.gc, plan.pieces)),
            dma((plan.gr, plan.chunks)),
            dma((plan.gr, plan.chunks)),
            dma((plan.gr, plan.chunks)),
            dma((plan.gr, plan.chunks)),
            dma((plan.gc, 1)),
            dma((plan.gc, 1)),
            dma((plan.gc,)),
            dma((plan.gc,)),
        ],
        compiler_params=pltpu.CompilerParams(
            collective_id=0, has_side_effects=True, vmem_limit_bytes=48 * 1024 * 1024
        ),
    )(
        pltpu.with_memory_space_constraint(demo, pltpu.HBM),
        pltpu.with_memory_space_constraint(rollout, pltpu.HBM),
    )
    return out[0], out[1], out[2]


def solution(mesh):
    rows_axis, cols_axis = mesh.shape["row"], mesh.shape["col"]

    def run(demo, rollout):
        blk = demo.shape[0] // (rows_axis * cols_axis)
        plan = Plan(rows_axis, cols_axis, blk, demo.shape[1])
        return jax.shard_map(
            functools.partial(body, plan),
            mesh=mesh,
            in_specs=(P(("row", "col"), None), P(("row", "col"), None)),
            out_specs=(P(("row", "col")), P(("row", "col")), P(("row", "col"))),
            check_vma=False,
        )(demo, rollout)

    return run
```
